32 devices in a mesh: row: 4 (over y, x), col: 8 (over z, core).
Axes of the slice: x: 2, y: 2, z: 4, core: 2. Of those that a mesh axis runs over, the one named last changes fastest.
Arguments:
- features: bfloat16 [4096, 512], P(('col', 'row')), may hold values from -6 to 6
- tile_vals: bfloat16 [4, 1024, 128, 128], P('row', 'col')
- tile_row: int32 [4, 1024], P('row', 'col'), may hold values from 0 to 7
- tile_col: int32 [4, 1024], P('row', 'col'), may hold values from 0 to 3
- tile_count: int32 [4, 8], P('row', 'col'), may hold values from 1 to 128, as said below
- node_type: int32 [4096], P(('row', 'col')), may hold values from 0 to 7
- type_gain: float32 [8, 512], replicated, may hold values from 0.1 to 1.9
- w_in: bfloat16 [512, 1024], replicated, may hold values from -0.25 to 0.25
- w_out: bfloat16 [1024, 512], replicated, may hold values from -0.1875 to 0.1875
- cotangent: bfloat16 [4096, 512], P(('row', 'col')), may hold values from -6 to 6
Outputs:
- mixed: bfloat16 [4096, 512], P(('row', 'col'))
- grad_x: float32 [4096, 512], P(('col', 'row'))
- grad_w_in: float32 [512, 1024], replicated
- grad_w_out: float32 [1024, 512], replicated
- grad_gain: float32 [8, 512], replicated
The draws below stay inside these ranges and needn't reach their ends.
Inputs may be any that keep to these rules, and one draw needn't show every extreme that they name: Slots 0 to tile_count - 1 of a grid cell's list are live; some grid cell has all 128 slots live in every draw.
All inputs are finite; a program needn't handle non-finite values.
Results may differ from the reference program's by a relative error of at most 0.0056.
Values may be sent and summed in bfloat16 or wider, within the bound.
No kernel may reach another device: no remote copies, remote signals or barrier semaphores. Data moves between devices by JAX's collectives and lax.ppermute only.
A program may use at most 128 MiB of HBM per device.

```python
import jax
import jax.numpy as jnp
from jax import lax

F = 512
HID = 1024
TYPES = 8
TILE = 128
TILES = 128
NODES = 4096
N_ROW = 4
N_COL = 8


def draw_tile_vals(key, part):
    base_key, keep_key = jax.random.split(jax.random.fold_in(key, 7), 2)
    shape = (N_ROW, N_COL * TILES, TILE, TILE)
    spread = (4.0 / (0.75 * TILE * TILES)) ** 0.5
    keeping = (jax.random.randint(keep_key, shape, 0, 4) > 0).astype(jnp.float32)
    values_drawn = jax.random.normal(base_key, shape, jnp.float32)
    return (values_drawn * keeping * spread).astype(jnp.bfloat16)


def draw_tile_count(key, part):
    first_key, second_key, pick_key = jax.random.split(jax.random.fold_in(key, 11), 3)
    first = jax.random.randint(first_key, (N_ROW * N_COL,), 1, TILES + 1)
    second = jax.random.randint(second_key, (N_ROW * N_COL,), 1, TILES + 1)
    counts = jnp.maximum(first * second // TILES, 1)
    chosen = jax.random.randint(pick_key, (), 0, N_ROW * N_COL)
    counts = jnp.where(jnp.arange(N_ROW * N_COL, dtype=jnp.int32) == chosen, TILES, counts)
    return counts.reshape(N_ROW, N_COL).astype(jnp.int32)


def set_ends(drawn, own_key, least, top_value):
    shape = drawn.shape
    place = [jax.random.randint(jax.random.fold_in(own_key, axis), (), 0, shape[axis]) for axis in range(len(shape))]
    drawn = drawn.at[tuple(place)].set(least)
    longest = shape.index(max(shape))
    place[longest] = (place[longest] + 1) % shape[longest]
    return drawn.at[tuple(place)].set(top_value)


def levels(key, extent, shards, smallest, top_value):
    def one(position, parts):
        steps = jax.random.uniform(jax.random.fold_in(jax.random.fold_in(key, 6), position), (parts,), jnp.float32, smallest / len(shards), top_value / len(shards))
        return jnp.repeat(jnp.exp(steps), extent[position] // parts).reshape((-1,) + (1,) * (len(extent) - position - 1))

    gain = one(*shards[0])
    for cut in shards[1:]:
        gain = gain * one(*cut)
    return gain


def noise(key, shape, width, reach, cuts=(), held_as=jnp.bfloat16):
    array = width * jax.random.normal(key, shape, jnp.float32)
    if cuts:
        array = array * levels(key, shape, cuts, -0.22, 0.18)
    return jnp.clip(array, -reach, reach).astype(held_as)


def setup_inputs(seed: int = 0) -> dict:
    seeds = jax.random.split(jax.random.key(seed), 11)
    features = noise(seeds[0], (NODES, F), 1.0, 6.0, ((0, 32),))
    tile_vals = draw_tile_vals(jax.random.fold_in(seeds[10], 71), 0)
    tile_row = set_ends(jax.random.randint(seeds[2], (N_ROW, N_COL * TILES), 0, N_COL), jax.random.fold_in(seeds[2], 1), 0, N_COL - 1).astype(jnp.int32)
    tile_col = set_ends(jax.random.randint(seeds[3], (N_ROW, N_COL * TILES), 0, N_ROW), jax.random.fold_in(seeds[3], 1), 0, N_ROW - 1).astype(jnp.int32)
    tile_count = draw_tile_count(jax.random.fold_in(seeds[10], 71), 0)
    node_type = set_ends(jax.random.randint(seeds[5], (NODES,), 0, TYPES), jax.random.fold_in(seeds[5], 1), 0, TYPES - 1).astype(jnp.int32)
    type_gain = jnp.clip(1.0 + 0.18 * jax.random.normal(seeds[6], (TYPES, F), jnp.float32), 0.1, 1.9)
    w_in = noise(seeds[7], (F, HID), F ** -0.5, 0.25)
    w_out = noise(seeds[8], (HID, F), HID ** -0.5, 0.1875)
    cotangent = noise(seeds[9], (NODES, F), 1.0, 6.0, ((0, 32),))
    return dict(features=features, tile_vals=tile_vals, tile_row=tile_row, tile_col=tile_col, tile_count=tile_count, node_type=node_type, type_gain=type_gain, w_in=w_in, w_out=w_out, cotangent=cotangent)


def reference(features, tile_vals, tile_row, tile_col, tile_count, node_type, type_gain, w_in, w_out, cotangent):
    total_nodes = TILE * N_ROW * N_COL
    blocks = N_COL * TILES // 16
    panels = features.reshape(N_COL, N_ROW, TILE, F).astype(jnp.float32)
    slot_ids = jnp.arange(N_COL * TILES, dtype=jnp.int32)
    owner_col = (slot_ids // TILES).astype(jnp.int32)
    owner_blocks = owner_col.reshape(blocks, 16)

    def living_slots(counts_row):
        return (slot_ids % TILES < counts_row[owner_col]).reshape(blocks, 16)

    def gather_rows(inputs):
        weights_row, rows_row, cols_row, counts_row = inputs
        living = living_slots(counts_row)

        def advance(totals, pieces):
            weights_now, row_ids, col_ids, owners, alive = pieces
            sources = panels[owners, col_ids]
            product = jnp.einsum('sab,sbf->saf', weights_now.astype(jnp.float32), sources, precision=lax.Precision.HIGHEST)
            product = jnp.where(alive[:, None, None], product, 0.0)
            return (totals.at[row_ids].add(product), None)
        start = jnp.zeros((N_COL, TILE, F), jnp.float32)
        totals, unused = lax.scan(advance, start, (weights_row.reshape(blocks, 16, TILE, TILE), rows_row.reshape(blocks, 16), cols_row.reshape(blocks, 16), owner_blocks, living))
        return totals
    aggregate = lax.map(gather_rows, (tile_vals, tile_row, tile_col, tile_count)).reshape(total_nodes, F)
    center = lax.optimization_barrier(jnp.mean(aggregate, axis=-1, keepdims=True))
    spread = lax.optimization_barrier(jnp.mean(jnp.square(aggregate - center), axis=-1, keepdims=True))
    inverse = lax.rsqrt(spread + 1e-05)
    normed = (aggregate - center) * inverse
    onehot = (node_type[:, None] == jnp.arange(TYPES, dtype=jnp.int32)[None, :]).astype(jnp.float32)
    gains = jnp.dot(onehot, type_gain, precision=lax.Precision.HIGHEST)
    scaled = (normed * gains).astype(jnp.bfloat16)
    hidden = jnp.dot(scaled, w_in, preferred_element_type=jnp.float32)
    activated = jax.nn.silu(hidden).astype(jnp.bfloat16)
    branch = jnp.dot(activated, w_out, preferred_element_type=jnp.float32)
    mixed = (aggregate + branch).astype(jnp.bfloat16)
    upstream = cotangent.astype(jnp.float32)
    grad_out_w = jnp.dot(activated.T, cotangent, preferred_element_type=jnp.float32)
    grad_act = jnp.dot(cotangent, w_out.T, preferred_element_type=jnp.float32)
    sigmoid_h = jax.nn.sigmoid(hidden)
    grad_hidden = (grad_act * sigmoid_h * (1.0 + hidden * (1.0 - sigmoid_h))).astype(jnp.bfloat16)
    grad_in_w = jnp.dot(scaled.T, grad_hidden, preferred_element_type=jnp.float32)
    grad_scaled = jnp.dot(grad_hidden, w_in.T, preferred_element_type=jnp.float32)
    grad_gain = jnp.dot(onehot.T, grad_scaled * normed, precision=lax.Precision.HIGHEST)
    grad_normed = grad_scaled * gains
    grad_agg = upstream + inverse * (grad_normed - lax.optimization_barrier(jnp.mean(grad_normed, axis=-1, keepdims=True)) - normed * lax.optimization_barrier(jnp.mean(grad_normed * normed, axis=-1, keepdims=True)))
    grad_rows = grad_agg.astype(jnp.bfloat16)
    grad_blocks = grad_rows.reshape(N_ROW, N_COL, TILE, F).astype(jnp.float32)

    def scatter_rows(totals, inputs):
        weights_row, rows_row, cols_row, counts_row, grads_row = inputs
        living = living_slots(counts_row)

        def advance(inner, pieces):
            weights_now, row_ids, col_ids, owners, alive = pieces
            sources = grads_row[row_ids]
            product = jnp.einsum('sab,saf->sbf', weights_now.astype(jnp.float32), sources, precision=lax.Precision.HIGHEST)
            product = jnp.where(alive[:, None, None], product, 0.0)
            return (inner.at[owners, col_ids].add(product), None)
        totals, unused = lax.scan(advance, totals, (weights_row.reshape(blocks, 16, TILE, TILE), rows_row.reshape(blocks, 16), cols_row.reshape(blocks, 16), owner_blocks, living))
        return (totals, None)
    start = jnp.zeros((N_COL, N_ROW, TILE, F), jnp.float32)
    grad_panels, unused = lax.scan(scatter_rows, start, (tile_vals, tile_row, tile_col, tile_count, grad_blocks))
    grad_x = grad_panels.reshape(total_nodes, F)
    factor = float(total_nodes) ** (-0.5)
    return (mixed, grad_x, grad_in_w * factor, grad_out_w * factor, grad_gain * factor)
```

```python
import jax
import jax.numpy as jnp
import numpy as np
from jax import lax
from jax.experimental import pallas as pl
from jax.experimental.pallas import tpu as pltpu
from jax.sharding import PartitionSpec as P

F = 512
TYPES = 8
TILE = 128
BF = jnp.bfloat16
FP = jnp.float32
AXES = ("row", "col")


def reversed_bits(value, bits):
    out = 0
    for b in range(bits):
        out |= ((value >> b) & 1) << (bits - 1 - b)
    return out


def exchange(x, rows, cols, row_masks, z_masks):
    pairs = []
    for r in range(rows):
        for c in range(cols):
            core = c & 1
            pairs.append((r * cols + c, (r ^ row_masks[core]) * cols + (c ^ (2 * z_masks[core]))))
    return lax.ppermute(x, AXES, pairs)


def swap_cores(x, rows, cols):
    return lax.ppermute(x, AXES, [(i, i ^ 1) for i in range(rows * cols)])


def rounded(x):
    return lax.reduce_precision(x, 8, 7).astype(BF)


def split(x):
    high = lax.reduce_precision(x, 8, 7)
    return jnp.concatenate([high.astype(BF), rounded(x - high)], axis=0)


def joined(x):
    x = x.astype(FP)
    return x[:TYPES] + x[TYPES:]


def build(tile_vals, tile_row, tile_col, live_count, row_order, col_order):
    slots = tile_vals.shape[0]
    n_r, n_c = row_order.shape[0], col_order.shape[0]
    half, wide = n_r // 2, n_c * TILE
    chunk = 16
    rounds = slots // chunk

    def kernel(count_ref, row_ref, col_ref, ro_ref, co_ref, vals_ref, near_ref, near_t_ref, far_ref, far_t_ref, total):
        step = pl.program_id(0)

        @pl.when(step == 0)
        def _():
            total[...] = jnp.zeros_like(total)

        first = step * chunk

        def add(s, carry):
            r, c = row_ref[first + s], col_ref[first + s]
            total[r, c] = total[r, c] + vals_ref[s].astype(FP)
            return carry

        lax.fori_loop(0, jnp.clip(count_ref[0] - first, 0, chunk), add, 0)

        @pl.when(step == rounds - 1)
        def _():
            for side, (out, out_t) in enumerate(((near_ref, near_t_ref), (far_ref, far_t_ref))):

                def emit(p, carry, side=side, out=out, out_t=out_t):
                    r = ro_ref[side * half + p]
                    at = pl.ds(pl.multiple_of(p * TILE, TILE), TILE)
                    for q in range(n_c):
                        value = total[r, co_ref[q]]
                        high = value.astype(BF)
                        out[at, q * TILE : (q + 1) * TILE] = high
                        out[at, wide + q * TILE : wide + (q + 1) * TILE] = (value - high.astype(FP)).astype(BF)
                        out_t[q * TILE : (q + 1) * TILE, at] = value.T.astype(BF)
                    return carry

                lax.fori_loop(0, half, emit, 0)

    dense = n_r * n_c * TILE * TILE
    plain = jax.ShapeDtypeStruct((half * TILE, 2 * wide), BF)
    turned = jax.ShapeDtypeStruct((wide, half * TILE), BF)
    return pl.pallas_call(
        kernel,
        out_shape=(plain, turned, plain, turned),
        grid_spec=pltpu.PrefetchScalarGridSpec(
            num_scalar_prefetch=5,
            grid=(rounds,),
            in_specs=[pl.BlockSpec((chunk, TILE, TILE), lambda i, *_: (i, 0, 0))],
            out_specs=tuple(pl.BlockSpec(x.shape, lambda i, *_: (0, 0)) for x in (plain, turned, plain, turned)),
            scratch_shapes=[pltpu.VMEM((n_r, n_c, TILE, TILE), FP)],
        ),
        compiler_params=pltpu.CompilerParams(vmem_limit_bytes=dense * 11 + 4 * 1024 * 1024),
        cost_estimate=pl.CostEstimate(
            flops=slots * TILE * TILE, bytes_accessed=slots * TILE * TILE * 2 + dense * 6, transcendentals=0
        ),
        name="build_dense",
    )(live_count, tile_row, tile_col, row_order, col_order, tile_vals)


def write_weights(near, far, core, first_order, second_order, factor):
    n_row = first_order.shape[0]
    lanes = near[0].shape[1]
    parts = len(near)
    span = near[0].shape[0] // n_row
    per = F // span

    def kernel(core_ref, f_ref, s_ref, *refs):
        mine, there, (in_ref, out_ref) = refs[:parts], refs[parts : 2 * parts], refs[2 * parts :]

        def put(sources, ref):
            for i, x in enumerate(sources):
                ref[:, i * lanes : (i + 1) * lanes] = x[...].astype(FP) * factor

        @pl.when(core_ref[0] == 0)
        def _():
            put(mine, in_ref)
            put(there, out_ref)

        @pl.when(core_ref[0] != 0)
        def _():
            put(there, in_ref)
            put(mine, out_ref)

    block = pl.BlockSpec((span, lanes), lambda q, *_: (q, 0))
    return pl.pallas_call(
        kernel,
        out_shape=(jax.ShapeDtypeStruct((F, 2 * F), FP), jax.ShapeDtypeStruct((2 * F, F), FP)),
        grid_spec=pltpu.PrefetchScalarGridSpec(
            num_scalar_prefetch=3,
            grid=(n_row,),
            in_specs=[block] * (2 * parts),
            out_specs=(
                pl.BlockSpec((span, F), lambda q, c, f, s: (f[q] % per, f[q] // per)),
                pl.BlockSpec((span, F), lambda q, c, f, s: (s[q], 0)),
            ),
        ),
        cost_estimate=pl.CostEstimate(flops=4 * F * F, bytes_accessed=24 * F * F, transcendentals=0),
        name="write_weights",
    )(core.reshape(1), first_order, second_order, *near, *far)


def tie(*arrays):
    return lax.optimization_barrier(arrays)


def shards(
    features,
    tile_vals,
    tile_row,
    tile_col,
    tile_count,
    node_type,
    type_gain,
    w_in,
    w_out,
    cotangent,
):
    n_row, n_col = lax.axis_size("row"), lax.axis_size("col")
    n_z = n_col // 2
    row_bits, z_bits = n_row.bit_length() - 1, n_z.bit_length() - 1
    total_nodes = TILE * n_row * n_col
    row, col = lax.axis_index("row"), lax.axis_index("col")
    core, z = col & 1, col >> 1

    def row_step(x, step):
        return exchange(x, n_row, n_col, (1 << step, 1 << (row_bits - 1 - step)), (0, 0))

    def z_step(x, step):
        return exchange(x, n_row, n_col, (0, 0), (1 << step, 1 << (z_bits - 1 - step)))

    def dot(a, b, dims):
        return lax.dot_general(a, b, (dims, ((), ())), preferred_element_type=FP)

    z_flip = jnp.array([reversed_bits(p, z_bits) for p in range(n_z)], jnp.int32)
    z_same = jnp.arange(n_z, dtype=jnp.int32)
    row_flip = row ^ jnp.array([reversed_bits(q, row_bits) for q in range(n_row)], jnp.int32)
    row_same = row ^ jnp.arange(n_row, dtype=jnp.int32)
    z_own = jnp.where(core == 0, z_same, z_flip)
    z_other = jnp.where(core == 0, z_flip, z_same)
    row_order = jnp.concatenate([2 * (z ^ z_own) + core, 2 * (z ^ z_other) + (1 - core)])
    col_order = jnp.where(core == 0, row_same, row_flip)

    near, near_t, far, far_t = build(tile_vals[0], tile_row[0], tile_col[0], tile_count[0], row_order, col_order)
    here, there = [features], []
    for step in range(row_bits):
        came = row_step(here[0] if step == 0 else jnp.concatenate(here, axis=0), step)
        there.append(swap_cores(here[-1], n_row, n_col))
        here.append(came)
    there.append(swap_cores(here[-1], n_row, n_col))
    far, far_t = swap_cores(far, n_row, n_col), swap_cores(far_t, n_row, n_col)

    total = dot(near, jnp.concatenate(here + here, axis=0), ((1,), (0,))) + dot(
        far, jnp.concatenate(there + there, axis=0), ((1,), (0,))
    )
    for step in reversed(range(z_bits)):
        mid = total.shape[0] // 2
        came = z_step(rounded(total[mid:]), step)
        total = total[:mid] + came.astype(FP)
    aggregate = total

    center = jnp.mean(aggregate, axis=-1, keepdims=True)
    spread = jnp.mean(jnp.square(aggregate - center), axis=-1, keepdims=True)
    inverse = lax.rsqrt(spread + 1e-05)
    normed = (aggregate - center) * inverse
    onehot = (node_type[:, None] == jnp.arange(TYPES, dtype=jnp.int32)[None, :]).astype(FP)
    gains = jnp.dot(onehot, type_gain, precision=lax.Precision.HIGHEST)
    scaled = (normed * gains).astype(BF)
    hidden = jnp.dot(scaled, w_in, preferred_element_type=FP)
    grad_act = dot(cotangent, w_out, ((1,), (1,)))
    sigmoid_h = jax.nn.sigmoid(hidden)
    activated = (hidden * sigmoid_h).astype(BF)
    grad_hidden = (grad_act * sigmoid_h * (1.0 + hidden * (1.0 - sigmoid_h))).astype(BF)

    for_in = jnp.concatenate([scaled, grad_hidden], axis=1)
    for_out = jnp.concatenate([cotangent, activated], axis=1)
    mine = jnp.where(core == 0, for_in, for_out)
    away = jnp.where(core == 0, for_out, for_in)
    away, activated, grad_hidden = tie(away, activated, grad_hidden)
    pairs = jnp.concatenate([mine, swap_cores(away, n_row, n_col)], axis=0)
    single, double = pairs[:, :F], pairs[:, F:]
    twice = jnp.concatenate([single, single], axis=1)
    left = jnp.where(core == 0, twice, double)
    right = jnp.where(core == 0, double, twice)
    wide = left.shape[1]
    span = wide // n_row
    parts = 2
    lanes = F // parts

    def weight_blocks(places, part):
        out = []
        for q in places:
            start = col_order[q] * span
            a = lax.dynamic_slice_in_dim(left, start, span, 1)
            b = lax.dynamic_slice_in_dim(right, (start // F) * F + part * lanes, lanes, 1)
            out.append(dot(a, b, ((0,), (0,))))
        return jnp.concatenate(out, axis=0)

    sums, outs = [None] * parts, [None] * parts
    for i in range(parts):
        outs[i] = rounded(weight_blocks(range(n_row // 2, n_row), i))
    *outs, activated, grad_hidden = tie(*outs, activated, grad_hidden)
    for i in range(parts):
        sums[i] = weight_blocks(range(n_row // 2), i)

    branch = jnp.dot(activated, w_out, preferred_element_type=FP)
    mixed = (aggregate + branch).astype(BF)
    grad_scaled = dot(grad_hidden, w_in, ((1,), (1,)))
    grad_gain = lax.dot_general(
        onehot, grad_scaled * normed, (((0,), (0,)), ((), ())), precision=lax.Precision.HIGHEST
    )
    grad_normed = grad_scaled * gains
    grad_agg = cotangent.astype(FP) + inverse * (
        grad_normed
        - jnp.mean(grad_normed, axis=-1, keepdims=True)
        - normed * jnp.mean(grad_normed * normed, axis=-1, keepdims=True)
    )
    grad_rows = grad_agg.astype(BF)

    gain = split(grad_gain)
    for step in range(z_bits):
        came = z_step(jnp.concatenate([grad_rows, gain], axis=0), step)
        size = grad_rows.shape[0]
        grad_rows = jnp.concatenate([grad_rows, came[:size]], axis=0)
        gain = split(joined(gain) + joined(came[size:]))
    came = swap_cores(rounded(dot(far_t, grad_rows, ((1,), (0,)))), n_row, n_col)
    low = dot(near_t, grad_rows, ((1,), (0,))) + came.astype(FP)
    for step in reversed(range(row_bits)):
        size = low.shape[0] // 2
        came = row_step(jnp.concatenate([rounded(low[size:]), gain], axis=0), step)
        gain = split(joined(gain) + joined(came[size:]))
        low = low[:size] + came[:size].astype(FP)
    grad_x = low
    factor = float(total_nodes) ** (-0.5)
    grad_gain = (joined(gain) + joined(swap_cores(gain, n_row, n_col))) * factor

    for step in reversed(range(row_bits)):
        for i in range(parts):
            mid = sums[i].shape[0] // 2
            sums[i] = sums[i] + row_step(outs[i], step).astype(FP)
            if step:
                sums[i], outs[i] = sums[i][:mid], rounded(sums[i][mid:])
    for step in range(z_bits):
        for i in range(parts):
            held = rounded(sums[i])
            sums[i] = held.astype(FP) + z_step(held, step).astype(FP)
    owns = [rounded(x) for x in sums]
    others = [[] for _ in range(parts)]
    for step in range(row_bits):
        for i in range(parts):
            came = row_step(owns[i], step)
            if step == row_bits - 1:
                others[i].append(swap_cores(owns[i], n_row, n_col))
                came, mixed, grad_x = tie(came, mixed, grad_x)
                others[i].append(swap_cores(came, n_row, n_col))
            owns[i] = jnp.concatenate([owns[i], came], axis=0)
    others = [jnp.concatenate(x, axis=0) for x in others]
    grad_w_in, grad_w_out = write_weights(owns, others, core, row_same, row_flip, factor)
    return mixed, grad_x, grad_w_in, grad_w_out, grad_gain


def solution(mesh):
    return jax.shard_map(
        shards,
        mesh=mesh,
        in_specs=(
            P(("col", "row"), None),
            P("row", "col", None, None),
            P("row", "col"),
            P("row", "col"),
            P("row", "col"),
            P(("row", "col")),
            P(),
            P(),
            P(),
            P(("row", "col"), None),
        ),
        out_specs=(P(("row", "col"), None), P(("col", "row"), None), P(), P(), P()),
        check_vma=False,
    )
```

```python
import jax
import jax.numpy as jnp
import numpy as np
from jax import lax
from jax.experimental import pallas as pl
from jax.experimental.pallas import tpu as pltpu
from jax.sharding import PartitionSpec as P

F = 512
TYPES = 8
TILE = 128
BF = jnp.bfloat16
FP = jnp.float32
AXES = ("row", "col")


def reversed_bits(value, bits):
    out = 0
    for b in range(bits):
        out |= ((value >> b) & 1) << (bits - 1 - b)
    return out


def exchange(x, rows, cols, row_masks, z_masks):
    pairs = []
    for r in range(rows):
        for c in range(cols):
            core = c & 1
            pairs.append((r * cols + c, (r ^ row_masks[core]) * cols + (c ^ (2 * z_masks[core]))))
    return lax.ppermute(x, AXES, pairs)


def swap_cores(x, rows, cols):
    return lax.ppermute(x, AXES, [(i, i ^ 1) for i in range(rows * cols)])


def rounded(x):
    return lax.reduce_precision(x, 8, 7).astype(BF)


def split(x):
    high = lax.reduce_precision(x, 8, 7)
    return jnp.concatenate([high.astype(BF), rounded(x - high)], axis=0)


def joined(x):
    x = x.astype(FP)
    return x[:TYPES] + x[TYPES:]


def build(tile_vals, tile_row, tile_col, tile_count, n_row, n_col):
    slots = tile_vals.shape[1]
    n_z = n_col // 2
    wide, half = n_row * TILE, n_z * TILE
    chunk = 16
    rounds = slots // chunk

    def kernel(count_ref, row_ref, col_ref, vals_ref, near_ref, far_ref, total, held, sems):
        copies = []
        for i in range(rounds):
            at = pl.ds(i * chunk, chunk)
            copies.append(pltpu.make_async_copy(vals_ref.at[0, at], held.at[at], sems.at[i]))
            copies[i].start()
        row, col = lax.axis_index("row"), lax.axis_index("col")
        core, z = col & 1, col >> 1
        total[...] = jnp.zeros_like(total)
        count = count_ref[0, 0]

        def add(s, carry):
            r, c = row_ref[0, s], col_ref[0, s]
            total[r, c] = total[r, c] + held[s].astype(FP)
            return carry

        for i in range(rounds):
            copies[i].wait()
            lax.fori_loop(i * chunk, jnp.clip(count, i * chunk, (i + 1) * chunk), add, 0)

        for side, out in enumerate((near_ref, far_ref)):
            whose = core ^ side

            def emit(p, carry, out=out, whose=whose):
                r = 2 * (z ^ jnp.where(whose == 0, p, reversed_bits(p, n_z.bit_length() - 1))) + whose
                at = pl.ds(pl.multiple_of(p * TILE, TILE), TILE)
                for q in range(n_row):
                    value = total[r, row ^ jnp.where(core == 0, q, reversed_bits(q, n_row.bit_length() - 1))]
                    high = value.astype(BF)
                    out[at, q * TILE : (q + 1) * TILE] = high
                    out[at, wide + q * TILE : wide + (q + 1) * TILE] = (value - high.astype(FP)).astype(BF)
                return carry

            lax.fori_loop(0, n_z, emit, 0)

    dense = n_row * n_col * TILE * TILE
    result = jax.ShapeDtypeStruct((half, 2 * wide), BF)
    smem = pl.BlockSpec(memory_space=pltpu.SMEM)
    return pl.pallas_call(
        kernel,
        out_shape=(result, result),
        in_specs=[smem, smem, smem, pl.BlockSpec(memory_space=pltpu.HBM)],
        scratch_shapes=[
            pltpu.VMEM((n_col, n_row, TILE, TILE), FP),
            pltpu.VMEM((slots, TILE, TILE), BF),
            pltpu.SemaphoreType.DMA((rounds,)),
        ],
        compiler_params=pltpu.CompilerParams(vmem_limit_bytes=dense * 9 + 8 * 1024 * 1024),
        cost_estimate=pl.CostEstimate(
            flops=slots * TILE * TILE, bytes_accessed=slots * TILE * TILE * 2 + dense * 4, transcendentals=0
        ),
        name="build_dense",
    )(tile_count, tile_row, tile_col, tile_vals)


def write_weights(near, far, held, first_place, n_row, factor):
    parts = len(near)
    rows, lanes = near[0].shape
    span = 2 * F // n_row
    places = rows // span
    per = F // span

    def kernel(*refs):
        mine, there = refs[:parts], refs[parts : 2 * parts]
        in_ref, out_ref, wide_in, wide_out, sems = refs[-5:]
        core, row = lax.axis_index("col") & 1, lax.axis_index("row")

        def put(sources, ref, at):
            for i, x in enumerate(sources):
                ref[at, i * lanes : (i + 1) * lanes] = x[at, :].astype(FP) * factor

        copies = []
        for j in range(places):
            q = first_place + j
            at = pl.ds(j * span, span)

            @pl.when(core == 0)
            def _(at=at):
                put(mine, wide_in, at)
                put(there, wide_out, at)

            @pl.when(core != 0)
            def _(at=at):
                put(there, wide_in, at)
                put(mine, wide_out, at)

            g = row ^ q
            to = in_ref.at[
                pl.ds(pl.multiple_of((g % per) * span, span), span), pl.ds(pl.multiple_of((g // per) * F, F), F)
            ]
            copies.append(pltpu.make_async_copy(wide_in.at[at], to, sems.at[2 * j]))
            copies[-1].start()
            g = row ^ reversed_bits(q, n_row.bit_length() - 1)
            to = out_ref.at[pl.ds(pl.multiple_of(g * span, span), span)]
            copies.append(pltpu.make_async_copy(wide_out.at[at], to, sems.at[2 * j + 1]))
            copies[-1].start()
        for copy in copies:
            copy.wait()

    vmem, hbm = pl.BlockSpec(memory_space=pltpu.VMEM), pl.BlockSpec(memory_space=pltpu.HBM)
    return pl.pallas_call(
        kernel,
        out_shape=(jax.ShapeDtypeStruct((F, 2 * F), FP), jax.ShapeDtypeStruct((2 * F, F), FP)),
        in_specs=[vmem] * (2 * parts) + [hbm] * len(held),
        out_specs=(hbm, hbm),
        input_output_aliases={2 * parts + i: i for i in range(len(held))},
        scratch_shapes=[
            pltpu.VMEM((rows, F), FP),
            pltpu.VMEM((rows, F), FP),
            pltpu.SemaphoreType.DMA((2 * places,)),
        ],
        compiler_params=pltpu.CompilerParams(vmem_limit_bytes=16 * 1024 * 1024),
        cost_estimate=pl.CostEstimate(flops=4 * rows * F, bytes_accessed=12 * rows * F, transcendentals=0),
        name="write_weights",
    )(*near, *far, *held)


def tie(*arrays):
    return lax.optimization_barrier(arrays)


def shards(
    features,
    tile_vals,
    tile_row,
    tile_col,
    tile_count,
    node_type,
    type_gain,
    w_in,
    w_out,
    cotangent,
):
    n_row, n_col = lax.axis_size("row"), lax.axis_size("col")
    n_z = n_col // 2
    row_bits, z_bits = n_row.bit_length() - 1, n_z.bit_length() - 1
    total_nodes = TILE * n_row * n_col
    row, col = lax.axis_index("row"), lax.axis_index("col")
    core, z = col & 1, col >> 1

    def row_step(x, step):
        return exchange(x, n_row, n_col, (1 << step, 1 << (row_bits - 1 - step)), (0, 0))

    def z_step(x, step):
        return exchange(x, n_row, n_col, (0, 0), (1 << step, 1 << (z_bits - 1 - step)))

    def dot(a, b, dims):
        return lax.dot_general(a, b, (dims, ((), ())), preferred_element_type=FP)

    def place(q):
        return row ^ jnp.where(core == 0, q, reversed_bits(q, row_bits))

    here, there = [features], []
    for step in range(row_bits):
        came = row_step(here[0] if step == 0 else jnp.concatenate(here, axis=0), step)
        if step == 0:
            came, tile_count = tie(came, tile_count)
        there.append(swap_cores(here[-1], n_row, n_col))
        here.append(came)
    there.append(swap_cores(here[-1], n_row, n_col))
    near, far = build(tile_vals, tile_row, tile_col, tile_count, n_row, n_col)
    far = swap_cores(far, n_row, n_col)

    total = dot(near, jnp.concatenate(here + here, axis=0), ((1,), (0,)))
    total, there[-1] = tie(total, there[-1])
    total = total + dot(far, jnp.concatenate(there + there, axis=0), ((1,), (0,)))
    for step in reversed(range(z_bits)):
        mid = total.shape[0] // 2
        came = z_step(rounded(total[mid:]), step)
        total = total[:mid] + came.astype(FP)
    aggregate = total

    center = jnp.mean(aggregate, axis=-1, keepdims=True)
    spread = jnp.mean(jnp.square(aggregate - center), axis=-1, keepdims=True)
    inverse = lax.rsqrt(spread + 1e-05)
    normed = (aggregate - center) * inverse
    onehot = (node_type[:, None] == jnp.arange(TYPES, dtype=jnp.int32)[None, :]).astype(FP)
    gains = jnp.dot(onehot, type_gain, precision=lax.Precision.HIGHEST)
    scaled = (normed * gains).astype(BF)
    hidden = jnp.dot(scaled, w_in, preferred_element_type=FP)
    grad_act = dot(cotangent, w_out, ((1,), (1,)))
    sigmoid_h = jax.nn.sigmoid(hidden)
    activated = (hidden * sigmoid_h).astype(BF)
    grad_hidden = (grad_act * sigmoid_h * (1.0 + hidden * (1.0 - sigmoid_h))).astype(BF)

    for_in = jnp.concatenate([scaled, grad_hidden], axis=1)
    for_out = jnp.concatenate([cotangent, activated], axis=1)
    mine = jnp.where(core == 0, for_in, for_out)
    away = jnp.where(core == 0, for_out, for_in)
    mine, grad_hidden = tie(mine, grad_hidden)
    met = swap_cores(away, n_row, n_col)

    grad_scaled = dot(grad_hidden, w_in, ((1,), (1,)))
    grad_gain = lax.dot_general(
        onehot, grad_scaled * normed, (((0,), (0,)), ((), ())), precision=lax.Precision.HIGHEST
    )
    grad_normed = grad_scaled * gains
    grad_agg = cotangent.astype(FP) + inverse * (
        grad_normed
        - jnp.mean(grad_normed, axis=-1, keepdims=True)
        - normed * jnp.mean(grad_normed * normed, axis=-1, keepdims=True)
    )
    grad_rows = grad_agg.astype(BF)
    gain = split(grad_gain)
    met, grad_rows, gain = tie(met, grad_rows, gain)
    pairs = jnp.concatenate([mine, met], axis=0)
    single, double = pairs[:, :F], pairs[:, F:]
    twice = jnp.concatenate([single, single], axis=1)
    left = jnp.where(core == 0, twice, double)
    right = jnp.where(core == 0, double, twice)
    wide = left.shape[1]
    span = wide // n_row
    parts = 2
    lanes = F // parts

    def weight_blocks(places, part):
        out = []
        for q in places:
            start = place(q) * span
            a = lax.dynamic_slice_in_dim(left, start, span, 1)
            b = lax.dynamic_slice_in_dim(right, (start // F) * F + part * lanes, lanes, 1)
            out.append(dot(a, b, ((0,), (0,))))
        return jnp.concatenate(out, axis=0)

    sums, outs = [None] * parts, [None] * parts
    for i in range(parts):
        outs[i] = rounded(weight_blocks(range(n_row // 2, n_row), i))
    *outs, activated = tie(*outs, activated)
    for i in range(parts):
        sums[i] = weight_blocks(range(n_row // 2), i)
    branch = jnp.dot(activated, w_out, preferred_element_type=FP)
    mixed = (aggregate + branch).astype(BF)

    for step in range(z_bits):
        came = z_step(jnp.concatenate([grad_rows, gain], axis=0), step)
        size = grad_rows.shape[0]
        grad_rows = jnp.concatenate([grad_rows, came[:size]], axis=0)
        gain = split(joined(gain) + joined(came[size:]))
    own = n_row * TILE
    came = swap_cores(rounded(dot(far[:, :own], grad_rows, ((0,), (0,)))), n_row, n_col)
    low = dot(near[:, :own], grad_rows, ((0,), (0,))) + came.astype(FP)
    for step in reversed(range(row_bits)):
        size = low.shape[0] // 2
        came = row_step(jnp.concatenate([rounded(low[size:]), gain], axis=0), step)
        gain = split(joined(gain) + joined(came[size:]))
        low = low[:size] + came[:size].astype(FP)
    grad_x = low
    factor = float(total_nodes) ** (-0.5)
    grad_gain = (joined(gain) + joined(swap_cores(gain, n_row, n_col))) * factor

    for step in reversed(range(row_bits)):
        for i in range(parts):
            mid = sums[i].shape[0] // 2
            sums[i] = sums[i] + row_step(outs[i], step).astype(FP)
            if step:
                sums[i], outs[i] = sums[i][:mid], rounded(sums[i][mid:])
    for step in range(z_bits):
        for i in range(parts):
            held = rounded(sums[i])
            sums[i] = held.astype(FP) + z_step(held, step).astype(FP)
    owns = [rounded(x) for x in sums]
    for step in range(row_bits - 1):
        for i in range(parts):
            owns[i] = jnp.concatenate([owns[i], row_step(owns[i], step)], axis=0)
    came = [row_step(x, row_bits - 1) for x in owns]
    others = [swap_cores(x, n_row, n_col) for x in owns]
    weights = write_weights(owns, others, [], 0, n_row, factor)
    *came, mixed, grad_x = tie(*came, mixed, grad_x)
    others = [swap_cores(x, n_row, n_col) for x in came]
    grad_w_in, grad_w_out = write_weights(came, others, weights, n_row // 2, n_row, factor)
    return mixed, grad_x, grad_w_in, grad_w_out, grad_gain


def solution(mesh):
    return jax.shard_map(
        shards,
        mesh=mesh,
        in_specs=(
            P(("col", "row"), None),
            P("row", "col", None, None),
            P("row", "col"),
            P("row", "col"),
            P("row", "col"),
            P(("row", "col")),
            P(),
            P(),
            P(),
            P(("row", "col"), None),
        ),
        out_specs=(P(("row", "col"), None), P(("col", "row"), None), P(), P(), P()),
        check_vma=False,
    )
```

```python
import jax
import jax.numpy as jnp
import numpy as np
from jax import lax
from jax.experimental import pallas as pl
from jax.experimental.pallas import tpu as pltpu
from jax.sharding import PartitionSpec as P

F = 512
TYPES = 8
TILE = 128
BF = jnp.bfloat16
FP = jnp.float32
AXES = ("row", "col")


def reversed_bits(value, bits):
    out = 0
    for b in range(bits):
        out |= ((value >> b) & 1) << (bits - 1 - b)
    return out


def exchange(x, rows, cols, row_masks, z_masks):
    pairs = []
    for r in range(rows):
        for c in range(cols):
            core = c & 1
            pairs.append((r * cols + c, (r ^ row_masks[core]) * cols + (c ^ (2 * z_masks[core]))))
    return lax.ppermute(x, AXES, pairs)


def swap_cores(x, rows, cols):
    return lax.ppermute(x, AXES, [(i, i ^ 1) for i in range(rows * cols)])


def rounded(x):
    return lax.reduce_precision(x, 8, 7).astype(BF)


def split(x):
    high = lax.reduce_precision(x, 8, 7)
    return jnp.concatenate([high.astype(BF), rounded(x - high)], axis=0)


def whole(x):
    x = x.astype(FP)
    return x[:TYPES] + x[TYPES:]


def build(tile_vals, tile_row, tile_col, tile_count, n_row, n_col):
    slots = tile_vals.shape[1]
    n_z = n_col // 2
    wide, half = n_row * TILE, n_z * TILE
    chunk = 16
    rounds = slots // chunk

    def kernel(
        count_ref, rows_ref, cols_ref, vals_ref, near_ref, far_ref, total, held, row_ref, col_ref, sems
    ):
        places = [
            pltpu.make_async_copy(rows_ref, row_ref, sems.at[rounds]),
            pltpu.make_async_copy(cols_ref, col_ref, sems.at[rounds + 1]),
        ]
        for copy in places:
            copy.start()
        copies = []
        for i in range(rounds):
            at = pl.ds(i * chunk, chunk)
            copies.append(pltpu.make_async_copy(vals_ref.at[0, at], held.at[at], sems.at[i]))
            copies[i].start()
        row, col = lax.axis_index("row"), lax.axis_index("col")
        core, z = col & 1, col >> 1
        total[...] = jnp.zeros_like(total)
        count = count_ref[0, 0]
        for copy in places:
            copy.wait()

        def add(s, carry):
            r, c = row_ref[0, s], col_ref[0, s]
            total[r, c] = total[r, c] + held[s].astype(FP)
            return carry

        for i in range(rounds):
            copies[i].wait()
            lax.fori_loop(i * chunk, jnp.clip(count, i * chunk, (i + 1) * chunk), add, 0)

        for side, out in enumerate((near_ref, far_ref)):
            whose = core ^ side

            def emit(p, carry, out=out, whose=whose):
                r = 2 * (z ^ jnp.where(whose == 0, p, reversed_bits(p, n_z.bit_length() - 1))) + whose
                at = pl.ds(pl.multiple_of(p * TILE, TILE), TILE)
                for q in range(n_row):
                    value = total[r, row ^ jnp.where(core == 0, q, reversed_bits(q, n_row.bit_length() - 1))]
                    high = value.astype(BF)
                    out[at, q * TILE : (q + 1) * TILE] = high
                    out[at, wide + q * TILE : wide + (q + 1) * TILE] = (value - high.astype(FP)).astype(BF)
                return carry

            lax.fori_loop(0, n_z, emit, 0)

    dense = n_row * n_col * TILE * TILE
    result = jax.ShapeDtypeStruct((half, 2 * wide), BF)
    return pl.pallas_call(
        kernel,
        out_shape=(result, result),
        in_specs=[pl.BlockSpec(memory_space=pltpu.SMEM)] + [pl.BlockSpec(memory_space=pl.ANY)] * 3,
        scratch_shapes=[
            pltpu.VMEM((n_col, n_row, TILE, TILE), FP),
            pltpu.VMEM((slots, TILE, TILE), BF),
            pltpu.SMEM((1, slots), jnp.int32),
            pltpu.SMEM((1, slots), jnp.int32),
            pltpu.SemaphoreType.DMA((rounds + 2,)),
        ],
        compiler_params=pltpu.CompilerParams(vmem_limit_bytes=dense * 9 + 8 * 1024 * 1024),
        cost_estimate=pl.CostEstimate(
            flops=slots * TILE * TILE, bytes_accessed=slots * TILE * TILE * 2 + dense * 4, transcendentals=0
        ),
        name="build_dense",
    )(tile_count, *(pltpu.with_memory_space_constraint(x, pltpu.HBM) for x in (tile_row, tile_col, tile_vals)))


def write_weights(near, far, held, gains, first_place, n_row, factor):
    parts = len(near)
    rows, lanes = near[0].shape
    span = 2 * F // n_row
    places = rows // span
    per = F // span

    def kernel(*refs):
        mine, there = refs[:parts], refs[parts : 2 * parts]
        in_ref, out_ref = refs[-5 - len(gains) // 2 :][:2]
        wide_in, wide_out, sems = refs[-3:]
        core, row = lax.axis_index("col") & 1, lax.axis_index("row")

        def put(sources, ref, at):
            for i, x in enumerate(sources):
                ref[at, i * lanes : (i + 1) * lanes] = x[at, :].astype(FP) * factor

        copies = []
        for j in range(places):
            q = first_place + j
            at = pl.ds(j * span, span)

            @pl.when(core == 0)
            def _(at=at):
                put(mine, wide_in, at)
                put(there, wide_out, at)

            @pl.when(core != 0)
            def _(at=at):
                put(there, wide_in, at)
                put(mine, wide_out, at)

            g = row ^ q
            to = in_ref.at[
                pl.ds(pl.multiple_of((g % per) * span, span), span), pl.ds(pl.multiple_of((g // per) * F, F), F)
            ]
            copies.append(pltpu.make_async_copy(wide_in.at[at], to, sems.at[2 * j]))
            copies[-1].start()
            g = row ^ reversed_bits(q, n_row.bit_length() - 1)
            to = out_ref.at[pl.ds(pl.multiple_of(g * span, span), span)]
            copies.append(pltpu.make_async_copy(wide_out.at[at], to, sems.at[2 * j + 1]))
            copies[-1].start()
        if gains:
            one, two = (x[...].astype(FP) for x in refs[2 * parts + len(held) :][:2])
            refs[-4][...] = ((one[:TYPES] + one[TYPES:]) + (two[:TYPES] + two[TYPES:])) * factor
        for copy in copies:
            copy.wait()

    vmem, hbm = pl.BlockSpec(memory_space=pltpu.VMEM), pl.BlockSpec(memory_space=pltpu.HBM)
    return pl.pallas_call(
        kernel,
        out_shape=(jax.ShapeDtypeStruct((F, 2 * F), FP), jax.ShapeDtypeStruct((2 * F, F), FP))
        + (jax.ShapeDtypeStruct((TYPES, F), FP),) * (len(gains) // 2),
        in_specs=[vmem] * (2 * parts) + [hbm] * len(held) + [vmem] * len(gains),
        out_specs=(hbm, hbm) + (vmem,) * (len(gains) // 2),
        input_output_aliases={2 * parts + i: i for i in range(len(held))},
        scratch_shapes=[
            pltpu.VMEM((rows, F), FP),
            pltpu.VMEM((rows, F), FP),
            pltpu.SemaphoreType.DMA((2 * places,)),
        ],
        compiler_params=pltpu.CompilerParams(vmem_limit_bytes=16 * 1024 * 1024),
        cost_estimate=pl.CostEstimate(flops=4 * rows * F, bytes_accessed=12 * rows * F, transcendentals=0),
        name="write_weights",
    )(*near, *far, *held, *gains)


def node_gradients(grad_hidden, w_in, aggregate, gains, cotangent, picked):
    rows = cotangent.shape[0]

    def kernel(gh_ref, w_ref, agg_ref, gains_ref, cot_ref, picked_ref, out_ref):
        aggregate = agg_ref[...]
        center = jnp.mean(aggregate, axis=-1, keepdims=True)
        spread = jnp.mean(jnp.square(aggregate - center), axis=-1, keepdims=True)
        inverse = lax.rsqrt(spread + 1e-05)
        normed = (aggregate - center) * inverse
        grad_scaled = lax.dot_general(
            gh_ref[...], w_ref[...], (((1,), (1,)), ((), ())), preferred_element_type=FP
        )
        grad_normed = grad_scaled * gains_ref[...]
        grad_agg = cot_ref[...].astype(FP) + inverse * (
            grad_normed
            - jnp.mean(grad_normed, axis=-1, keepdims=True)
            - normed * jnp.mean(grad_normed * normed, axis=-1, keepdims=True)
        )
        out_ref[:rows] = grad_agg.astype(BF)
        gain = jnp.dot(
            picked_ref[...], grad_scaled * normed, precision=lax.Precision.HIGHEST, preferred_element_type=FP
        )
        high = gain.astype(BF).astype(FP)
        out_ref[rows:] = jnp.concatenate([high, gain - high], axis=0).astype(BF)

    return pl.pallas_call(
        kernel,
        out_shape=jax.ShapeDtypeStruct((rows + 2 * TYPES, F), BF),
        in_specs=[pl.BlockSpec(memory_space=pltpu.VMEM)] * 6,
        out_specs=pl.BlockSpec(memory_space=pltpu.VMEM),
        compiler_params=pltpu.CompilerParams(vmem_limit_bytes=8 * 1024 * 1024),
        cost_estimate=pl.CostEstimate(flops=4 * rows * F * F, bytes_accessed=4 * F * F, transcendentals=rows),
        name="node_gradients",
    )(grad_hidden, w_in, aggregate, gains, cotangent, picked)


def weight_blocks(mine, met, places, n_row, parts, dtype, through=()):
    span = 2 * F // n_row
    per = F // span
    lanes = F // parts
    rows = len(places) * span

    def kernel(mine_ref, met_ref, *refs):
        outs = refs[len(through) : len(through) + parts]
        core, row = lax.axis_index("col") & 1, lax.axis_index("row")

        def block(left, right):
            total = None
            for ref in (mine_ref, met_ref):
                term = lax.dot_general(
                    ref[:, left], ref[:, right], (((0,), (0,)), ((), ())), preferred_element_type=FP
                )
                total = term if total is None else total + term
            return total

        def put(j, value):
            for i, out in enumerate(outs):
                out[j * span : (j + 1) * span, :] = value[:, i * lanes : (i + 1) * lanes].astype(dtype)

        for j, q in enumerate(places):

            @pl.when(core == 0)
            def _(j=j, q=q):
                g = row ^ q
                left = pl.ds(pl.multiple_of((g % per) * span, span), span)
                right = pl.ds(pl.multiple_of(F + (g // per) * F, F), F)
                put(j, block(left, right))

            @pl.when(core != 0)
            def _(j=j, q=q):
                g = row ^ reversed_bits(q, n_row.bit_length() - 1)
                left = pl.ds(pl.multiple_of(F + g * span, span), span)
                put(j, block(left, slice(0, F)))

    return pl.pallas_call(
        kernel,
        out_shape=tuple(jax.ShapeDtypeStruct((rows, lanes), dtype) for _ in range(parts))
        + tuple(jax.ShapeDtypeStruct(x.shape, x.dtype) for x in through),
        in_specs=[pl.BlockSpec(memory_space=pltpu.VMEM)] * 2 + [pl.BlockSpec(memory_space=pl.ANY)] * len(through),
        out_specs=(pl.BlockSpec(memory_space=pltpu.VMEM),) * parts
        + (pl.BlockSpec(memory_space=pl.ANY),) * len(through),
        input_output_aliases={2 + i: parts + i for i in range(len(through))},
        compiler_params=pltpu.CompilerParams(vmem_limit_bytes=8 * 1024 * 1024),
        cost_estimate=pl.CostEstimate(
            flops=4 * TILE * rows * F, bytes_accessed=8 * TILE * F + 4 * rows * F, transcendentals=0
        ),
        name="weight_blocks",
    )(mine, met, *through)


def mix(aggregate, activated, w_out, after):
    def kernel(agg_ref, act_ref, w_ref, after_ref, out_ref):
        branch = jnp.dot(act_ref[...], w_ref[...], preferred_element_type=FP)
        out_ref[...] = (agg_ref[...] + branch).astype(BF)

    vmem = pl.BlockSpec(memory_space=pltpu.VMEM)
    return pl.pallas_call(
        kernel,
        out_shape=jax.ShapeDtypeStruct(aggregate.shape, BF),
        in_specs=[vmem, vmem, vmem, pl.BlockSpec(memory_space=pl.ANY)],
        out_specs=vmem,
        compiler_params=pltpu.CompilerParams(vmem_limit_bytes=8 * 1024 * 1024),
        cost_estimate=pl.CostEstimate(flops=0, bytes_accessed=0, transcendentals=0),
        name="mix",
    )(aggregate, activated, w_out, after)


def small_call(kernel, name, outs, operands, after=()):
    n, m = len(operands), len(after)

    def body(*refs):
        kernel(*refs[:n], *refs[n + m :])

    moved = sum(x.size * x.dtype.itemsize for x in (*operands, *outs))
    vmem = pl.BlockSpec(memory_space=pltpu.VMEM)
    return pl.pallas_call(
        body,
        out_shape=tuple(outs),
        in_specs=[vmem] * n + [pl.BlockSpec(memory_space=pl.ANY)] * m,
        out_specs=(vmem,) * len(outs),
        compiler_params=pltpu.CompilerParams(vmem_limit_bytes=2 * moved + 4 * 1024 * 1024),
        cost_estimate=pl.CostEstimate(flops=0, bytes_accessed=0, transcendentals=0),
        name=name,
    )(*operands, *after)


def added(keep, came, halves, after):
    n, lanes = keep.shape
    half = n // 2

    def kernel(keep_ref, came_ref, *outs):
        if halves:
            outs[0][...] = (keep_ref[half:].astype(FP) + came_ref[half:].astype(FP)).astype(BF)
            outs[1][...] = keep_ref[:half].astype(FP) + came_ref[:half].astype(FP)
        else:
            outs[0][...] = (keep_ref[...].astype(FP) + came_ref[...].astype(FP)).astype(BF)

    if halves:
        outs = (jax.ShapeDtypeStruct((half, lanes), BF), jax.ShapeDtypeStruct((half, lanes), FP))
    else:
        outs = (jax.ShapeDtypeStruct((n, lanes), BF),)
    return small_call(kernel, "added", outs, (keep, came), after)


def node_values(keep, came, gains, w_in, w_out, cotangent):
    n = keep.shape[0]

    def kernel(keep_ref, came_ref, gains_ref, w_in_ref, w_out_ref, cot_ref, agg_ref, mine_ref, away_ref, act_ref, gh_ref):
        aggregate = keep_ref[...] + came_ref[...].astype(FP)
        agg_ref[...] = aggregate
        center = jnp.mean(aggregate, axis=-1, keepdims=True)
        spread = jnp.mean(jnp.square(aggregate - center), axis=-1, keepdims=True)
        inverse = lax.rsqrt(spread + 1e-05)
        scaled = ((aggregate - center) * inverse * gains_ref[...]).astype(BF)
        cot = cot_ref[...]
        grad_act = lax.dot_general(cot, w_out_ref[...], (((1,), (1,)), ((), ())), preferred_element_type=FP)
        hidden = jnp.dot(scaled, w_in_ref[...], preferred_element_type=FP)
        sigmoid_h = jax.nn.sigmoid(hidden)
        activated = (hidden * sigmoid_h).astype(BF)
        grad_hidden = (grad_act * sigmoid_h * (1.0 + hidden * (1.0 - sigmoid_h))).astype(BF)
        act_ref[...] = activated
        gh_ref[...] = grad_hidden

        def put(for_in, for_out):
            for_in[:, :F] = scaled
            for_in[:, F:] = grad_hidden
            for_out[:, :F] = cot
            for_out[:, F:] = activated

        first = lax.axis_index("col") & 1 == 0

        @pl.when(first)
        def _():
            put(mine_ref, away_ref)

        @pl.when(jnp.logical_not(first))
        def _():
            put(away_ref, mine_ref)

    outs = (jax.ShapeDtypeStruct((n, F), FP),) + tuple(jax.ShapeDtypeStruct((n, w * F), BF) for w in (3, 3, 2, 2))
    return small_call(kernel, "node_values", outs, (keep, came, gains, w_in, w_out, cotangent))


def shards(
    features,
    tile_vals,
    tile_row,
    tile_col,
    tile_count,
    node_type,
    type_gain,
    w_in,
    w_out,
    cotangent,
):
    n_row, n_col = lax.axis_size("row"), lax.axis_size("col")
    n_z = n_col // 2
    row_bits, z_bits = n_row.bit_length() - 1, n_z.bit_length() - 1
    total_nodes = TILE * n_row * n_col
    row, col = lax.axis_index("row"), lax.axis_index("col")
    core, z = col & 1, col >> 1

    def row_step(x, step):
        return exchange(x, n_row, n_col, (1 << step, 1 << (row_bits - 1 - step)), (0, 0))

    def z_step(x, step):
        return exchange(x, n_row, n_col, (0, 0), (1 << step, 1 << (z_bits - 1 - step)))

    def dot(a, b, dims):
        return lax.dot_general(a, b, (dims, ((), ())), preferred_element_type=FP)

    def place(q):
        return row ^ jnp.where(core == 0, q, reversed_bits(q, row_bits))

    here = [features]
    for q in range(1, n_row):
        here.append(exchange(features, n_row, n_col, (q, reversed_bits(q, row_bits)), (0, 0)))
    there = [swap_cores(features, n_row, n_col), swap_cores(jnp.concatenate(here[1:], axis=0), n_row, n_col)]
    near, far = build(tile_vals, tile_row, tile_col, tile_count, n_row, n_col)
    far = swap_cores(far, n_row, n_col)
    onehot = (node_type[:, None] == jnp.arange(TYPES, dtype=jnp.int32)[None, :]).astype(FP)
    gains = jnp.dot(onehot, type_gain, precision=lax.Precision.HIGHEST)

    mid = near.shape[0] // 2
    here, there = jnp.concatenate(here + here, axis=0), jnp.concatenate(there + there, axis=0)
    sent = rounded(dot(near[mid:], here, ((1,), (0,))) + dot(far[mid:], there, ((1,), (0,))))
    total = dot(near[:mid], here, ((1,), (0,))) + dot(far[:mid], there, ((1,), (0,)))
    for step in reversed(range(z_bits)):
        came = z_step(sent, step)
        if step:
            sent, total = added(total, came, True, ())
    aggregate, mine, away, activated, grad_hidden = node_values(total, came, gains, w_in, w_out, cotangent)

    met = swap_cores(away, n_row, n_col)
    node_rows = node_gradients(grad_hidden, w_in, aggregate, gains, cotangent, onehot.T)
    parts = 2
    sent = list(weight_blocks(mine, met, range(n_row // 2, n_row), n_row, parts, BF))
    *sums, node_rows = weight_blocks(mine, met, range(n_row // 2), n_row, parts, FP, (node_rows,))

    grad_rows, gain = node_rows[:TILE], node_rows[TILE:]
    for step in range(z_bits):
        came = z_step(jnp.concatenate([grad_rows, gain], axis=0), step)
        size = grad_rows.shape[0]
        grad_rows = jnp.concatenate([grad_rows, came[:size]], axis=0)
        gain = split(whole(gain) + whole(came[size:]))
    own = n_row * TILE
    came = swap_cores(rounded(dot(far[:, :own], grad_rows, ((0,), (0,)))), n_row, n_col)
    low = dot(near[:, :own], grad_rows, ((0,), (0,))) + came.astype(FP)
    for step in reversed(range(row_bits)):
        size = low.shape[0] // 2
        came = row_step(jnp.concatenate([rounded(low[size:]), gain], axis=0), step)
        gain = split(whole(gain) + whole(came[size:]))
        low = low[:size] + came[:size].astype(FP)
    grad_x = low

    mixed = None
    for step in reversed(range(row_bits)):
        for i in range(parts):
            mid = sums[i].shape[0] // 2
            came = row_step(sent[i], step)
            if mixed is None:
                mixed = mix(aggregate, activated, w_out, came)
            sums[i] = sums[i] + came.astype(FP)
            if step:
                sums[i], sent[i] = sums[i][:mid], rounded(sums[i][mid:])
    for step in range(z_bits):
        for i in range(parts):
            held = rounded(sums[i])
            sums[i] = held.astype(FP) + z_step(held, step).astype(FP)
    sent = [rounded(x) for x in sums]
    for step in range(row_bits - 1):
        for i in range(parts):
            sent[i] = jnp.concatenate([sent[i], row_step(sent[i], step)], axis=0)
    came = [row_step(x, row_bits - 1) for x in sent]

    factor = float(total_nodes) ** (-0.5)
    others = [swap_cores(x, n_row, n_col) for x in sent]
    weights = write_weights(sent, others, [], [], 0, n_row, factor)
    others = [swap_cores(x, n_row, n_col) for x in came]
    grad_w_in, grad_w_out, grad_gain = write_weights(
        came, others, weights, [gain, swap_cores(gain, n_row, n_col)], n_row // 2, n_row, factor
    )
    return mixed, grad_x, grad_w_in, grad_w_out, grad_gain


def solution(mesh):
    return jax.shard_map(
        shards,
        mesh=mesh,
        in_specs=(
            P(("col", "row"), None),
            P("row", "col", None, None),
            P("row", "col"),
            P("row", "col"),
            P("row", "col"),
            P(("row", "col")),
            P(),
            P(),
            P(),
            P(("row", "col"), None),
        ),
        out_specs=(P(("row", "col"), None), P(("col", "row"), None), P(), P(), P()),
        check_vma=False,
    )
```

```python
import jax
import jax.numpy as jnp
import numpy as np
from jax import lax
from jax.experimental import pallas as pl
from jax.experimental.pallas import tpu as pltpu
from jax.sharding import PartitionSpec as P

F = 512
TYPES = 8
TILE = 128
BF = jnp.bfloat16
FP = jnp.float32
AXES = ("row", "col")


def reversed_bits(value, bits):
    out = 0
    for b in range(bits):
        out |= ((value >> b) & 1) << (bits - 1 - b)
    return out


def exchange(x, rows, cols, row_masks, z_masks):
    pairs = []
    for r in range(rows):
        for c in range(cols):
            core = c & 1
            pairs.append((r * cols + c, (r ^ row_masks[core]) * cols + (c ^ (2 * z_masks[core]))))
    return lax.ppermute(x, AXES, pairs)


def swap_cores(x, rows, cols):
    return lax.ppermute(x, AXES, [(i, i ^ 1) for i in range(rows * cols)])


def rounded(x):
    return lax.reduce_precision(x, 8, 7).astype(BF)


def split(x):
    high = lax.reduce_precision(x, 8, 7)
    return jnp.concatenate([high.astype(BF), rounded(x - high)], axis=0)


def whole(x):
    x = x.astype(FP)
    return x[:TYPES] + x[TYPES:]


def build(tile_vals, tile_row, tile_col, tile_count, n_row, n_col):
    slots = tile_vals.shape[1]
    n_z = n_col // 2
    wide, half = n_row * TILE, n_z * TILE
    chunk = 16
    rounds = slots // chunk

    def kernel(
        count_ref, rows_ref, cols_ref, vals_ref, near_ref, far_ref, total, held, row_ref, col_ref, sems
    ):
        places = [
            pltpu.make_async_copy(rows_ref, row_ref, sems.at[rounds]),
            pltpu.make_async_copy(cols_ref, col_ref, sems.at[rounds + 1]),
        ]
        for copy in places:
            copy.start()
        copies = []
        for i in range(rounds):
            at = pl.ds(i * chunk, chunk)
            copies.append(pltpu.make_async_copy(vals_ref.at[0, at], held.at[at], sems.at[i]))
            copies[i].start()
        row, col = lax.axis_index("row"), lax.axis_index("col")
        core, z = col & 1, col >> 1
        total[...] = jnp.zeros_like(total)
        count = count_ref[0, 0]
        for copy in places:
            copy.wait()

        def add(s, carry):
            r, c = row_ref[0, s], col_ref[0, s]
            total[r, c] = total[r, c] + held[s].astype(FP)
            return carry

        for i in range(rounds):
            copies[i].wait()
            lax.fori_loop(i * chunk, jnp.clip(count, i * chunk, (i + 1) * chunk), add, 0)

        for side, out in enumerate((near_ref, far_ref)):
            whose = core ^ side

            def emit(p, carry, out=out, whose=whose):
                r = 2 * (z ^ jnp.where(whose == 0, p, reversed_bits(p, n_z.bit_length() - 1))) + whose
                at = pl.ds(pl.multiple_of(p * TILE, TILE), TILE)
                for q in range(n_row):
                    value = total[r, row ^ jnp.where(core == 0, q, reversed_bits(q, n_row.bit_length() - 1))]
                    high = value.astype(BF)
                    out[at, q * TILE : (q + 1) * TILE] = high
                    out[at, wide + q * TILE : wide + (q + 1) * TILE] = (value - high.astype(FP)).astype(BF)
                return carry

            lax.fori_loop(0, n_z, emit, 0)

    dense = n_row * n_col * TILE * TILE
    result = jax.ShapeDtypeStruct((half, 2 * wide), BF)
    return pl.pallas_call(
        kernel,
        out_shape=(result, result),
        in_specs=[pl.BlockSpec(memory_space=pltpu.SMEM)] + [pl.BlockSpec(memory_space=pl.ANY)] * 3,
        scratch_shapes=[
            pltpu.VMEM((n_col, n_row, TILE, TILE), FP),
            pltpu.VMEM((slots, TILE, TILE), BF),
            pltpu.SMEM((1, slots), jnp.int32),
            pltpu.SMEM((1, slots), jnp.int32),
            pltpu.SemaphoreType.DMA((rounds + 2,)),
        ],
        compiler_params=pltpu.CompilerParams(vmem_limit_bytes=dense * 9 + 8 * 1024 * 1024),
        cost_estimate=pl.CostEstimate(
            flops=slots * TILE * TILE, bytes_accessed=slots * TILE * TILE * 2 + dense * 4, transcendentals=0
        ),
        name="build_dense",
    )(tile_count, *(pltpu.with_memory_space_constraint(x, pltpu.HBM) for x in (tile_row, tile_col, tile_vals)))


def write_weights(near, far, held, gains, first_place, first_lane, n_row, factor, through=()):
    parts = len(near)
    rows, lanes = near[0].shape
    width = parts * lanes
    span = 2 * F // n_row
    places = rows // span
    per = F // span
    n_gain = len(gains) // 2

    def kernel(*refs):
        mine, there = refs[:parts], refs[parts : 2 * parts]
        outs = refs[2 * parts + len(held) + len(gains) + len(through) :]
        in_ref, out_ref = outs[:2]
        wide_in, wide_out, sems = refs[-3:]
        core, row = lax.axis_index("col") & 1, lax.axis_index("row")

        def put(sources, ref, at):
            for i, x in enumerate(sources):
                ref[at, i * lanes : (i + 1) * lanes] = x[at, :].astype(FP) * factor

        copies = []
        for j in range(places):
            q = first_place + j
            at = pl.ds(j * span, span)

            @pl.when(core == 0)
            def _(at=at):
                put(mine, wide_in, at)
                put(there, wide_out, at)

            @pl.when(core != 0)
            def _(at=at):
                put(there, wide_in, at)
                put(mine, wide_out, at)

            g = row ^ q
            to = in_ref.at[
                pl.ds(pl.multiple_of((g % per) * span, span), span),
                pl.ds(pl.multiple_of((g // per) * F + first_lane, TILE), width),
            ]
            copies.append(pltpu.make_async_copy(wide_in.at[at], to, sems.at[2 * j]))
            copies[-1].start()
            g = row ^ reversed_bits(q, n_row.bit_length() - 1)
            to = out_ref.at[pl.ds(pl.multiple_of(g * span, span), span), pl.ds(first_lane, width)]
            copies.append(pltpu.make_async_copy(wide_out.at[at], to, sems.at[2 * j + 1]))
            copies[-1].start()
        if gains:
            one, two = (x[...].astype(FP) for x in refs[2 * parts + len(held) :][:2])
            outs[2][...] = ((one[:TYPES] + one[TYPES:]) + (two[:TYPES] + two[TYPES:])) * factor
        for copy in copies:
            copy.wait()

    vmem, hbm = pl.BlockSpec(memory_space=pltpu.VMEM), pl.BlockSpec(memory_space=pltpu.HBM)
    keep = pl.BlockSpec(memory_space=pl.ANY)
    before = 2 * parts + len(held) + len(gains)
    aliases = {2 * parts + i: i for i in range(len(held))}
    aliases.update({before + i: 2 + n_gain + i for i in range(len(through))})
    return pl.pallas_call(
        kernel,
        out_shape=(jax.ShapeDtypeStruct((F, 2 * F), FP), jax.ShapeDtypeStruct((2 * F, F), FP))
        + (jax.ShapeDtypeStruct((TYPES, F), FP),) * n_gain
        + tuple(jax.ShapeDtypeStruct(x.shape, x.dtype) for x in through),
        in_specs=[vmem] * (2 * parts) + [hbm] * len(held) + [vmem] * len(gains) + [keep] * len(through),
        out_specs=(hbm, hbm) + (vmem,) * n_gain + (keep,) * len(through),
        input_output_aliases=aliases,
        scratch_shapes=[
            pltpu.VMEM((rows, width), FP),
            pltpu.VMEM((rows, width), FP),
            pltpu.SemaphoreType.DMA((2 * places,)),
        ],
        compiler_params=pltpu.CompilerParams(vmem_limit_bytes=16 * 1024 * 1024),
        cost_estimate=pl.CostEstimate(flops=0, bytes_accessed=0, transcendentals=0),
        name="write_weights",
    )(*near, *far, *held, *gains, *through)


def node_gradients(grad_hidden, w_in, aggregate, gains, cotangent, picked):
    rows = cotangent.shape[0]

    def kernel(gh_ref, w_ref, agg_ref, gains_ref, cot_ref, picked_ref, out_ref):
        aggregate = agg_ref[...]
        center = jnp.mean(aggregate, axis=-1, keepdims=True)
        spread = jnp.mean(jnp.square(aggregate - center), axis=-1, keepdims=True)
        inverse = lax.rsqrt(spread + 1e-05)
        normed = (aggregate - center) * inverse
        grad_scaled = lax.dot_general(
            gh_ref[...], w_ref[...], (((1,), (1,)), ((), ())), preferred_element_type=FP
        )
        grad_normed = grad_scaled * gains_ref[...]
        grad_agg = cot_ref[...].astype(FP) + inverse * (
            grad_normed
            - jnp.mean(grad_normed, axis=-1, keepdims=True)
            - normed * jnp.mean(grad_normed * normed, axis=-1, keepdims=True)
        )
        out_ref[:rows] = grad_agg.astype(BF)
        gain = jnp.dot(
            picked_ref[...], grad_scaled * normed, precision=lax.Precision.HIGHEST, preferred_element_type=FP
        )
        high = gain.astype(BF).astype(FP)
        out_ref[rows:] = jnp.concatenate([high, gain - high], axis=0).astype(BF)

    return pl.pallas_call(
        kernel,
        out_shape=jax.ShapeDtypeStruct((rows + 2 * TYPES, F), BF),
        in_specs=[pl.BlockSpec(memory_space=pltpu.VMEM)] * 6,
        out_specs=pl.BlockSpec(memory_space=pltpu.VMEM),
        compiler_params=pltpu.CompilerParams(vmem_limit_bytes=8 * 1024 * 1024),
        cost_estimate=pl.CostEstimate(flops=4 * rows * F * F, bytes_accessed=4 * F * F, transcendentals=rows),
        name="node_gradients",
    )(grad_hidden, w_in, aggregate, gains, cotangent, picked)


def weight_blocks(mine, met, places, n_row, lanes, dtype, through=()):
    span = 2 * F // n_row
    per = F // span
    rows = len(places) * span
    parts = len(lanes)
    low, high = lanes[0][0], lanes[-1][0] + lanes[-1][1]

    def kernel(mine_ref, met_ref, *refs):
        outs = refs[len(through) : len(through) + parts]
        core, row = lax.axis_index("col") & 1, lax.axis_index("row")

        def block(left, right):
            total = None
            for ref in (mine_ref, met_ref):
                term = lax.dot_general(
                    ref[:, left], ref[:, right], (((0,), (0,)), ((), ())), preferred_element_type=FP
                )
                total = term if total is None else total + term
            return total

        def put(j, value):
            for (start, size), out in zip(lanes, outs):
                out[j * span : (j + 1) * span, :] = value[:, start - low : start - low + size].astype(dtype)

        for j, q in enumerate(places):

            @pl.when(core == 0)
            def _(j=j, q=q):
                g = row ^ q
                left = pl.ds(pl.multiple_of((g % per) * span, span), span)
                right = pl.ds(pl.multiple_of(F + low + (g // per) * F, TILE), high - low)
                put(j, block(left, right))

            @pl.when(core != 0)
            def _(j=j, q=q):
                g = row ^ reversed_bits(q, n_row.bit_length() - 1)
                left = pl.ds(pl.multiple_of(F + g * span, span), span)
                put(j, block(left, slice(low, high)))

    return pl.pallas_call(
        kernel,
        out_shape=tuple(jax.ShapeDtypeStruct((rows, size), dtype) for _, size in lanes)
        + tuple(jax.ShapeDtypeStruct(x.shape, x.dtype) for x in through),
        in_specs=[pl.BlockSpec(memory_space=pltpu.VMEM)] * 2 + [pl.BlockSpec(memory_space=pl.ANY)] * len(through),
        out_specs=(pl.BlockSpec(memory_space=pltpu.VMEM),) * parts
        + (pl.BlockSpec(memory_space=pl.ANY),) * len(through),
        input_output_aliases={2 + i: parts + i for i in range(len(through))},
        compiler_params=pltpu.CompilerParams(vmem_limit_bytes=8 * 1024 * 1024),
        cost_estimate=pl.CostEstimate(
            flops=4 * TILE * rows * (high - low), bytes_accessed=8 * TILE * F + 4 * rows * F, transcendentals=0
        ),
        name="weight_blocks",
    )(mine, met, *through)


def mix(aggregate, activated, w_out, after):
    def kernel(agg_ref, act_ref, w_ref, after_ref, out_ref):
        branch = jnp.dot(act_ref[...], w_ref[...], preferred_element_type=FP)
        out_ref[...] = (agg_ref[...] + branch).astype(BF)

    vmem = pl.BlockSpec(memory_space=pltpu.VMEM)
    return pl.pallas_call(
        kernel,
        out_shape=jax.ShapeDtypeStruct(aggregate.shape, BF),
        in_specs=[vmem, vmem, vmem, pl.BlockSpec(memory_space=pl.ANY)],
        out_specs=vmem,
        compiler_params=pltpu.CompilerParams(vmem_limit_bytes=8 * 1024 * 1024),
        cost_estimate=pl.CostEstimate(flops=0, bytes_accessed=0, transcendentals=0),
        name="mix",
    )(aggregate, activated, w_out, after)


def small_call(kernel, name, outs, operands, after=()):
    n, m = len(operands), len(after)

    def body(*refs):
        kernel(*refs[:n], *refs[n + m :])

    moved = sum(x.size * x.dtype.itemsize for x in (*operands, *outs))
    vmem = pl.BlockSpec(memory_space=pltpu.VMEM)
    return pl.pallas_call(
        body,
        out_shape=tuple(outs),
        in_specs=[vmem] * n + [pl.BlockSpec(memory_space=pl.ANY)] * m,
        out_specs=(vmem,) * len(outs),
        compiler_params=pltpu.CompilerParams(vmem_limit_bytes=2 * moved + 4 * 1024 * 1024),
        cost_estimate=pl.CostEstimate(flops=0, bytes_accessed=0, transcendentals=0),
        name=name,
    )(*operands, *after)


def added(keep, came, halves, after):
    n, lanes = keep.shape
    half = n // 2

    def kernel(keep_ref, came_ref, *outs):
        if halves:
            outs[0][...] = (keep_ref[half:].astype(FP) + came_ref[half:].astype(FP)).astype(BF)
            outs[1][...] = keep_ref[:half].astype(FP) + came_ref[:half].astype(FP)
        else:
            outs[0][...] = (keep_ref[...].astype(FP) + came_ref[...].astype(FP)).astype(BF)

    if halves:
        outs = (jax.ShapeDtypeStruct((half, lanes), BF), jax.ShapeDtypeStruct((half, lanes), FP))
    else:
        outs = (jax.ShapeDtypeStruct((n, lanes), BF),)
    return small_call(kernel, "added", outs, (keep, came), after)


def node_values(keep, came, gains, w_in, w_out, cotangent):
    n = keep.shape[0]

    def kernel(keep_ref, came_ref, gains_ref, w_in_ref, w_out_ref, cot_ref, agg_ref, mine_ref, away_ref, act_ref, gh_ref):
        aggregate = keep_ref[...] + came_ref[...].astype(FP)
        agg_ref[...] = aggregate
        center = jnp.mean(aggregate, axis=-1, keepdims=True)
        spread = jnp.mean(jnp.square(aggregate - center), axis=-1, keepdims=True)
        inverse = lax.rsqrt(spread + 1e-05)
        scaled = ((aggregate - center) * inverse * gains_ref[...]).astype(BF)
        cot = cot_ref[...]
        grad_act = lax.dot_general(cot, w_out_ref[...], (((1,), (1,)), ((), ())), preferred_element_type=FP)
        hidden = jnp.dot(scaled, w_in_ref[...], preferred_element_type=FP)
        sigmoid_h = jax.nn.sigmoid(hidden)
        activated = (hidden * sigmoid_h).astype(BF)
        grad_hidden = (grad_act * sigmoid_h * (1.0 + hidden * (1.0 - sigmoid_h))).astype(BF)
        act_ref[...] = activated
        gh_ref[...] = grad_hidden

        def put(for_in, for_out):
            for_in[:, :F] = scaled
            for_in[:, F:] = grad_hidden
            for_out[:, :F] = cot
            for_out[:, F:] = activated

        first = lax.axis_index("col") & 1 == 0

        @pl.when(first)
        def _():
            put(mine_ref, away_ref)

        @pl.when(jnp.logical_not(first))
        def _():
            put(away_ref, mine_ref)

    outs = (jax.ShapeDtypeStruct((n, F), FP),) + tuple(jax.ShapeDtypeStruct((n, w * F), BF) for w in (3, 3, 2, 2))
    return small_call(kernel, "node_values", outs, (keep, came, gains, w_in, w_out, cotangent))


def joined(held, came, after):
    n, lanes = held.shape

    def kernel(held_ref, came_ref, out_ref):
        out_ref[:n] = held_ref[...]
        out_ref[n:] = came_ref[...]

    outs = (jax.ShapeDtypeStruct((2 * n, lanes), BF),)
    return small_call(kernel, "joined", outs, (held, came), after)[0]


def shards(
    features,
    tile_vals,
    tile_row,
    tile_col,
    tile_count,
    node_type,
    type_gain,
    w_in,
    w_out,
    cotangent,
):
    n_row, n_col = lax.axis_size("row"), lax.axis_size("col")
    n_z = n_col // 2
    row_bits, z_bits = n_row.bit_length() - 1, n_z.bit_length() - 1
    total_nodes = TILE * n_row * n_col
    row, col = lax.axis_index("row"), lax.axis_index("col")
    core, z = col & 1, col >> 1

    def row_step(x, step):
        return exchange(x, n_row, n_col, (1 << step, 1 << (row_bits - 1 - step)), (0, 0))

    def z_step(x, step):
        return exchange(x, n_row, n_col, (0, 0), (1 << step, 1 << (z_bits - 1 - step)))

    def dot(a, b, dims):
        return lax.dot_general(a, b, (dims, ((), ())), preferred_element_type=FP)

    def place(q):
        return row ^ jnp.where(core == 0, q, reversed_bits(q, row_bits))

    here = [features]
    for q in range(1, n_row):
        here.append(exchange(features, n_row, n_col, (q, reversed_bits(q, row_bits)), (0, 0)))
    there = [swap_cores(features, n_row, n_col), swap_cores(jnp.concatenate(here[1:], axis=0), n_row, n_col)]
    near, far = build(tile_vals, tile_row, tile_col, tile_count, n_row, n_col)
    far = swap_cores(far, n_row, n_col)
    onehot = (node_type[:, None] == jnp.arange(TYPES, dtype=jnp.int32)[None, :]).astype(FP)
    gains = jnp.dot(onehot, type_gain, precision=lax.Precision.HIGHEST)

    mid = near.shape[0] // 2
    here, there = jnp.concatenate(here + here, axis=0), jnp.concatenate(there + there, axis=0)
    sent = rounded(dot(near[mid:], here, ((1,), (0,))) + dot(far[mid:], there, ((1,), (0,))))
    total = dot(near[:mid], here, ((1,), (0,))) + dot(far[:mid], there, ((1,), (0,)))
    for step in reversed(range(z_bits)):
        came = z_step(sent, step)
        if step:
            sent, total = added(total, came, True, ())
    aggregate, mine, away, activated, grad_hidden = node_values(total, came, gains, w_in, w_out, cotangent)

    met = swap_cores(away, n_row, n_col)
    node_rows = node_gradients(grad_hidden, w_in, aggregate, gains, cotangent, onehot.T)
    parts = 2
    lanes = [(i * F // parts, F // parts) for i in range(parts)]
    ahead, behind = range(n_row // 2, n_row), range(n_row // 2)
    first, node_rows = weight_blocks(mine, met, ahead, n_row, lanes[:1], BF, (node_rows,))
    sent = [first] + [weight_blocks(mine, met, ahead, n_row, [x], BF)[0] for x in lanes[1:]]
    sums = list(weight_blocks(mine, met, behind, n_row, lanes, FP))

    grad_rows, gain = node_rows[:TILE], node_rows[TILE:]
    for step in range(z_bits):
        came = z_step(jnp.concatenate([grad_rows, gain], axis=0), step)
        size = grad_rows.shape[0]
        grad_rows = jnp.concatenate([grad_rows, came[:size]], axis=0)
        gain = split(whole(gain) + whole(came[size:]))
    own = n_row * TILE
    came = swap_cores(rounded(dot(far[:, :own], grad_rows, ((0,), (0,)))), n_row, n_col)
    low = dot(near[:, :own], grad_rows, ((0,), (0,))) + came.astype(FP)
    marks = []
    for step in reversed(range(row_bits)):
        size = low.shape[0] // 2
        marks.append(jnp.concatenate([rounded(low[size:]), gain], axis=0))
        came = row_step(marks[-1], step)
        gain = split(whole(gain) + whole(came[size:]))
        low = low[:size] + came[:size].astype(FP)
    grad_x = low

    mixed = None
    for step in reversed(range(row_bits)):
        for i in range(parts):
            mid = sums[i].shape[0] // 2
            came = row_step(sent[i], step)
            if mixed is None:
                mixed = mix(aggregate, activated, w_out, came)
            sums[i] = sums[i] + came.astype(FP)
            if step:
                sums[i], sent[i] = sums[i][:mid], rounded(sums[i][mid:])
    for step in range(z_bits):
        for i in range(parts):
            if step == 0:
                sent[i] = rounded(sums[i])
            came = z_step(sent[i], step)
            if step == 0 and i == parts - 1:
                sent[i] = added(sent[i], came, False, marks[:1])[0]
            else:
                sent[i] = rounded(sent[i].astype(FP) + came.astype(FP))
    for step in range(row_bits - 1):
        for i in range(parts):
            came = row_step(sent[i], step)
            if step == row_bits - 2:
                sent[i] = joined(sent[i], came, sent[:i] + (marks[-1:] if i == parts - 1 else []))
            else:
                sent[i] = jnp.concatenate([sent[i], came], axis=0)
    came = [row_step(x, row_bits - 1) for x in sent]

    factor = float(total_nodes) ** (-0.5)
    others = [swap_cores(x, n_row, n_col) for x in sent]
    gains = [gain, swap_cores(gain, n_row, n_col)]
    *weights, came[0] = write_weights(sent, others, [], [], 0, 0, n_row, factor, came[:1])
    others = [swap_cores(x, n_row, n_col) for x in came]
    *weights, grad_gain = write_weights(came, others, weights, gains, n_row // 2, 0, n_row, factor)
    grad_w_in, grad_w_out = weights
    return mixed, grad_x, grad_w_in, grad_w_out, grad_gain


def solution(mesh):
    return jax.shard_map(
        shards,
        mesh=mesh,
        in_specs=(
            P(("col", "row"), None),
            P("row", "col", None, None),
            P("row", "col"),
            P("row", "col"),
            P("row", "col"),
            P(("row", "col")),
            P(),
            P(),
            P(),
            P(("row", "col"), None),
        ),
        out_specs=(P(("row", "col"), None), P(("col", "row"), None), P(), P(), P()),
        check_vma=False,
    )
```

```python
import jax
import jax.numpy as jnp
import numpy as np
from jax import lax
from jax.experimental import pallas as pl
from jax.experimental.pallas import tpu as pltpu
from jax.sharding import PartitionSpec as P

F = 512
TYPES = 8
TILE = 128
BF = jnp.bfloat16
FP = jnp.float32
AXES = ("row", "col")


def reversed_bits(value, bits):
    out = 0
    for b in range(bits):
        out |= ((value >> b) & 1) << (bits - 1 - b)
    return out


def exchange(x, rows, cols, row_masks, z_masks):
    pairs = []
    for r in range(rows):
        for c in range(cols):
            core = c & 1
            pairs.append((r * cols + c, (r ^ row_masks[core]) * cols + (c ^ (2 * z_masks[core]))))
    return lax.ppermute(x, AXES, pairs)


def swap_cores(x, rows, cols):
    return lax.ppermute(x, AXES, [(i, i ^ 1) for i in range(rows * cols)])


def rounded(x):
    return lax.reduce_precision(x, 8, 7).astype(BF)


def split(x):
    high = lax.reduce_precision(x, 8, 7)
    return jnp.concatenate([high.astype(BF), rounded(x - high)], axis=0)


def whole(x):
    x = x.astype(FP)
    return x[:TYPES] + x[TYPES:]


def build(tile_vals, tile_row, tile_col, tile_count, n_row, n_col):
    slots = tile_vals.shape[1]
    n_z = n_col // 2
    wide, half = n_row * TILE, n_z * TILE
    chunk = 16
    rounds = slots // chunk

    def kernel(
        count_ref, rows_ref, cols_ref, vals_ref, near_ref, far_ref, total, held, row_ref, col_ref, sems
    ):
        places = [
            pltpu.make_async_copy(rows_ref, row_ref, sems.at[rounds]),
            pltpu.make_async_copy(cols_ref, col_ref, sems.at[rounds + 1]),
        ]
        for copy in places:
            copy.start()
        copies = []
        for i in range(rounds):
            at = pl.ds(i * chunk, chunk)
            copies.append(pltpu.make_async_copy(vals_ref.at[0, at], held.at[at], sems.at[i]))
            copies[i].start()
        row, col = lax.axis_index("row"), lax.axis_index("col")
        core, z = col & 1, col >> 1
        total[...] = jnp.zeros_like(total)
        count = count_ref[0, 0]
        for copy in places:
            copy.wait()

        def add(s, carry):
            r, c = row_ref[0, s], col_ref[0, s]
            total[r, c] = total[r, c] + held[s].astype(FP)
            return carry

        for i in range(rounds):
            copies[i].wait()
            lax.fori_loop(i * chunk, jnp.clip(count, i * chunk, (i + 1) * chunk), add, 0)

        for side, out in enumerate((near_ref, far_ref)):
            whose = core ^ side

            def emit(p, carry, out=out, whose=whose):
                r = 2 * (z ^ jnp.where(whose == 0, p, reversed_bits(p, n_z.bit_length() - 1))) + whose
                at = pl.ds(pl.multiple_of(p * TILE, TILE), TILE)
                for q in range(n_row):
                    value = total[r, row ^ jnp.where(core == 0, q, reversed_bits(q, n_row.bit_length() - 1))]
                    high = value.astype(BF)
                    out[at, q * TILE : (q + 1) * TILE] = high
                    out[at, wide + q * TILE : wide + (q + 1) * TILE] = (value - high.astype(FP)).astype(BF)
                return carry

            lax.fori_loop(0, n_z, emit, 0)

    dense = n_row * n_col * TILE * TILE
    result = jax.ShapeDtypeStruct((half, 2 * wide), BF)
    return pl.pallas_call(
        kernel,
        out_shape=(result, result),
        in_specs=[pl.BlockSpec(memory_space=pltpu.SMEM)] + [pl.BlockSpec(memory_space=pl.ANY)] * 3,
        scratch_shapes=[
            pltpu.VMEM((n_col, n_row, TILE, TILE), FP),
            pltpu.VMEM((slots, TILE, TILE), BF),
            pltpu.SMEM((1, slots), jnp.int32),
            pltpu.SMEM((1, slots), jnp.int32),
            pltpu.SemaphoreType.DMA((rounds + 2,)),
        ],
        compiler_params=pltpu.CompilerParams(vmem_limit_bytes=dense * 9 + 8 * 1024 * 1024),
        cost_estimate=pl.CostEstimate(
            flops=slots * TILE * TILE, bytes_accessed=slots * TILE * TILE * 2 + dense * 4, transcendentals=0
        ),
        name="build_dense",
    )(tile_count, *(pltpu.with_memory_space_constraint(x, pltpu.HBM) for x in (tile_row, tile_col, tile_vals)))


def write_weights(near, far, held, gains, first_place, first_lane, n_row, factor, through=(), after=()):
    parts = len(near)
    rows = near[0].shape[0]
    sizes = [x.shape[1] for x in near]
    width = sum(sizes)
    span = 2 * F // n_row
    places = rows // span
    per = F // span
    n_gain = len(gains) // 2

    def kernel(*refs):
        mine, there = refs[:parts], refs[parts : 2 * parts]
        outs = refs[2 * parts + len(held) + len(gains) + len(through) + len(after) :]
        in_ref, out_ref = outs[:2]
        wide_in, wide_out, sems = refs[-3:]
        core, row = lax.axis_index("col") & 1, lax.axis_index("row")

        def put(sources, ref, at):
            start = 0
            for x, size in zip(sources, sizes):
                ref[at, start : start + size] = x[at, :].astype(FP) * factor
                start += size

        copies = []
        for j in range(places):
            q = first_place + j
            at = pl.ds(j * span, span)

            @pl.when(core == 0)
            def _(at=at):
                put(mine, wide_in, at)
                put(there, wide_out, at)

            @pl.when(core != 0)
            def _(at=at):
                put(there, wide_in, at)
                put(mine, wide_out, at)

            g = row ^ q
            to = in_ref.at[
                pl.ds(pl.multiple_of((g % per) * span, span), span),
                pl.ds(pl.multiple_of((g // per) * F + first_lane, TILE), width),
            ]
            copies.append(pltpu.make_async_copy(wide_in.at[at], to, sems.at[2 * j]))
            copies[-1].start()
            g = row ^ reversed_bits(q, n_row.bit_length() - 1)
            to = out_ref.at[pl.ds(pl.multiple_of(g * span, span), span), pl.ds(first_lane, width)]
            copies.append(pltpu.make_async_copy(wide_out.at[at], to, sems.at[2 * j + 1]))
            copies[-1].start()
        if gains:
            one, two = (x[...].astype(FP) for x in refs[2 * parts + len(held) :][:2])
            outs[2][...] = ((one[:TYPES] + one[TYPES:]) + (two[:TYPES] + two[TYPES:])) * factor
        for copy in copies:
            copy.wait()

    vmem, hbm = pl.BlockSpec(memory_space=pltpu.VMEM), pl.BlockSpec(memory_space=pltpu.HBM)
    keep = pl.BlockSpec(memory_space=pl.ANY)
    before = 2 * parts + len(held) + len(gains)
    aliases = {2 * parts + i: i for i in range(len(held))}
    aliases.update({before + i: 2 + n_gain + i for i in range(len(through))})
    return pl.pallas_call(
        kernel,
        out_shape=(jax.ShapeDtypeStruct((F, 2 * F), FP), jax.ShapeDtypeStruct((2 * F, F), FP))
        + (jax.ShapeDtypeStruct((TYPES, F), FP),) * n_gain
        + tuple(jax.ShapeDtypeStruct(x.shape, x.dtype) for x in through),
        in_specs=[vmem] * (2 * parts) + [hbm] * len(held) + [vmem] * len(gains) + [keep] * (len(through) + len(after)),
        out_specs=(hbm, hbm) + (vmem,) * n_gain + (keep,) * len(through),
        input_output_aliases=aliases,
        scratch_shapes=[
            pltpu.VMEM((rows, width), FP),
            pltpu.VMEM((rows, width), FP),
            pltpu.SemaphoreType.DMA((2 * places,)),
        ],
        compiler_params=pltpu.CompilerParams(vmem_limit_bytes=16 * 1024 * 1024),
        cost_estimate=pl.CostEstimate(flops=0, bytes_accessed=0, transcendentals=0),
        name="write_weights",
    )(*near, *far, *held, *gains, *through, *after)


def node_gradients(grad_hidden, w_in, aggregate, gains, cotangent, picked):
    rows = cotangent.shape[0]

    def kernel(gh_ref, w_ref, agg_ref, gains_ref, cot_ref, picked_ref, out_ref):
        aggregate = agg_ref[...]
        center = jnp.mean(aggregate, axis=-1, keepdims=True)
        spread = jnp.mean(jnp.square(aggregate - center), axis=-1, keepdims=True)
        inverse = lax.rsqrt(spread + 1e-05)
        normed = (aggregate - center) * inverse
        grad_scaled = lax.dot_general(
            gh_ref[...], w_ref[...], (((1,), (1,)), ((), ())), preferred_element_type=FP
        )
        grad_normed = grad_scaled * gains_ref[...]
        grad_agg = cot_ref[...].astype(FP) + inverse * (
            grad_normed
            - jnp.mean(grad_normed, axis=-1, keepdims=True)
            - normed * jnp.mean(grad_normed * normed, axis=-1, keepdims=True)
        )
        out_ref[:rows] = grad_agg.astype(BF)
        gain = jnp.dot(
            picked_ref[...], grad_scaled * normed, precision=lax.Precision.HIGHEST, preferred_element_type=FP
        )
        high = gain.astype(BF).astype(FP)
        out_ref[rows:] = jnp.concatenate([high, gain - high], axis=0).astype(BF)

    return pl.pallas_call(
        kernel,
        out_shape=jax.ShapeDtypeStruct((rows + 2 * TYPES, F), BF),
        in_specs=[pl.BlockSpec(memory_space=pltpu.VMEM)] * 6,
        out_specs=pl.BlockSpec(memory_space=pltpu.VMEM),
        compiler_params=pltpu.CompilerParams(vmem_limit_bytes=8 * 1024 * 1024),
        cost_estimate=pl.CostEstimate(flops=4 * rows * F * F, bytes_accessed=4 * F * F, transcendentals=rows),
        name="node_gradients",
    )(grad_hidden, w_in, aggregate, gains, cotangent, picked)


def weight_blocks(mine, met, places, n_row, lanes, dtype, through=(), mixing=()):
    span = 2 * F // n_row
    per = F // span
    rows = len(places) * span
    parts = len(lanes)
    extra = 1 if mixing else 0
    low, high = lanes[0][0], lanes[-1][0] + lanes[-1][1]

    def kernel(mine_ref, met_ref, *refs):
        outs = refs[len(through) + len(mixing) :][:parts]
        core, row = lax.axis_index("col") & 1, lax.axis_index("row")
        if mixing:
            aggregate, activated, w_out = refs[len(through) : len(through) + 3]
            held, sem = refs[-2:]
            branch = jnp.dot(activated[...], w_out[...], preferred_element_type=FP)
            held[...] = (aggregate[...] + branch).astype(BF)
            copy = pltpu.make_async_copy(held, refs[-3], sem)
            copy.start()

        def block(left, right):
            total = None
            for ref in (mine_ref, met_ref):
                term = lax.dot_general(
                    ref[:, left], ref[:, right], (((0,), (0,)), ((), ())), preferred_element_type=FP
                )
                total = term if total is None else total + term
            return total

        def put(j, value):
            for (start, size), out in zip(lanes, outs):
                out[j * span : (j + 1) * span, :] = value[:, start - low : start - low + size].astype(dtype)

        for j, q in enumerate(places):

            @pl.when(core == 0)
            def _(j=j, q=q):
                g = row ^ q
                left = pl.ds(pl.multiple_of((g % per) * span, span), span)
                right = pl.ds(pl.multiple_of(F + low + (g // per) * F, TILE), high - low)
                put(j, block(left, right))

            @pl.when(core != 0)
            def _(j=j, q=q):
                g = row ^ reversed_bits(q, n_row.bit_length() - 1)
                left = pl.ds(pl.multiple_of(F + g * span, span), span)
                put(j, block(left, slice(low, high)))

        if mixing:
            copy.wait()

    vmem, keep = pl.BlockSpec(memory_space=pltpu.VMEM), pl.BlockSpec(memory_space=pl.ANY)
    mixed = [jax.ShapeDtypeStruct(mixing[0].shape, BF)] if mixing else []
    return pl.pallas_call(
        kernel,
        out_shape=tuple(jax.ShapeDtypeStruct((rows, size), dtype) for _, size in lanes)
        + tuple(jax.ShapeDtypeStruct(x.shape, x.dtype) for x in (*through, *mixed)),
        in_specs=[vmem] * 2 + [keep] * len(through) + [vmem] * len(mixing),
        out_specs=(vmem,) * parts + (keep,) * len(through) + (pl.BlockSpec(memory_space=pltpu.HBM),) * extra,
        input_output_aliases={2 + i: parts + i for i in range(len(through))},
        scratch_shapes=[pltpu.VMEM(x.shape, BF) for x in mixed] + [pltpu.SemaphoreType.DMA] * extra,
        compiler_params=pltpu.CompilerParams(vmem_limit_bytes=8 * 1024 * 1024),
        cost_estimate=pl.CostEstimate(
            flops=4 * TILE * rows * (high - low), bytes_accessed=8 * TILE * F + 4 * rows * F, transcendentals=0
        ),
        name="weight_blocks",
    )(mine, met, *through, *mixing)


def small_call(kernel, name, outs, operands, after=()):
    n, m = len(operands), len(after)

    def body(*refs):
        kernel(*refs[:n], *refs[n + m :])

    moved = sum(x.size * x.dtype.itemsize for x in (*operands, *outs))
    vmem = pl.BlockSpec(memory_space=pltpu.VMEM)
    return pl.pallas_call(
        body,
        out_shape=tuple(outs),
        in_specs=[vmem] * n + [pl.BlockSpec(memory_space=pl.ANY)] * m,
        out_specs=(vmem,) * len(outs),
        compiler_params=pltpu.CompilerParams(vmem_limit_bytes=2 * moved + 4 * 1024 * 1024),
        cost_estimate=pl.CostEstimate(flops=0, bytes_accessed=0, transcendentals=0),
        name=name,
    )(*operands, *after)


def added(keep, came, halves, after):
    n, lanes = keep.shape
    half = n // 2

    def kernel(keep_ref, came_ref, *outs):
        if halves:
            outs[0][...] = (keep_ref[half:].astype(FP) + came_ref[half:].astype(FP)).astype(BF)
            outs[1][...] = keep_ref[:half].astype(FP) + came_ref[:half].astype(FP)
        else:
            outs[0][...] = (keep_ref[...].astype(FP) + came_ref[...].astype(FP)).astype(BF)

    if halves:
        outs = (jax.ShapeDtypeStruct((half, lanes), BF), jax.ShapeDtypeStruct((half, lanes), FP))
    else:
        outs = (jax.ShapeDtypeStruct((n, lanes), BF),)
    return small_call(kernel, "added", outs, (keep, came), after)


def node_values(keep, came, gains, w_in, w_out, cotangent):
    n = keep.shape[0]

    def kernel(keep_ref, came_ref, gains_ref, w_in_ref, w_out_ref, cot_ref, agg_ref, mine_ref, away_ref, act_ref, gh_ref):
        aggregate = keep_ref[...] + came_ref[...].astype(FP)
        agg_ref[...] = aggregate
        center = jnp.mean(aggregate, axis=-1, keepdims=True)
        spread = jnp.mean(jnp.square(aggregate - center), axis=-1, keepdims=True)
        inverse = lax.rsqrt(spread + 1e-05)
        scaled = ((aggregate - center) * inverse * gains_ref[...]).astype(BF)
        cot = cot_ref[...]
        grad_act = lax.dot_general(cot, w_out_ref[...], (((1,), (1,)), ((), ())), preferred_element_type=FP)
        hidden = jnp.dot(scaled, w_in_ref[...], preferred_element_type=FP)
        sigmoid_h = jax.nn.sigmoid(hidden)
        activated = (hidden * sigmoid_h).astype(BF)
        grad_hidden = (grad_act * sigmoid_h * (1.0 + hidden * (1.0 - sigmoid_h))).astype(BF)
        act_ref[...] = activated
        gh_ref[...] = grad_hidden

        def put(for_in, for_out):
            for_in[:, :F] = scaled
            for_in[:, F:] = grad_hidden
            for_out[:, :F] = cot
            for_out[:, F:] = activated

        first = lax.axis_index("col") & 1 == 0

        @pl.when(first)
        def _():
            put(mine_ref, away_ref)

        @pl.when(jnp.logical_not(first))
        def _():
            put(away_ref, mine_ref)

    outs = (jax.ShapeDtypeStruct((n, F), FP),) + tuple(jax.ShapeDtypeStruct((n, w * F), BF) for w in (3, 3, 2, 2))
    return small_call(kernel, "node_values", outs, (keep, came, gains, w_in, w_out, cotangent))


def joined(held, came, after):
    n, lanes = held.shape

    def kernel(held_ref, came_ref, out_ref):
        out_ref[:n] = held_ref[...]
        out_ref[n:] = came_ref[...]

    outs = (jax.ShapeDtypeStruct((2 * n, lanes), BF),)
    return small_call(kernel, "joined", outs, (held, came), after)[0]


def product(block, rows, first):
    n = block.shape[0] - first

    def kernel(block_ref, rows_ref, out_ref):
        out_ref[...] = jnp.dot(block_ref[first:], rows_ref[...], preferred_element_type=FP)

    return small_call(kernel, "product", (jax.ShapeDtypeStruct((n, F), FP),), (block, rows))[0]


def stacked(pieces, after):
    n = sum(x.shape[0] for x in pieces)

    def kernel(*refs):
        out_ref = refs[-1]
        at = 0
        for x in refs[:-1]:
            out_ref[at : at + x.shape[0]] = x[...]
            out_ref[n + at : n + at + x.shape[0]] = x[...]
            at += x.shape[0]

    return small_call(kernel, "stacked", (jax.ShapeDtypeStruct((2 * n, F), BF),), tuple(pieces), after)[0]


def shards(
    features,
    tile_vals,
    tile_row,
    tile_col,
    tile_count,
    node_type,
    type_gain,
    w_in,
    w_out,
    cotangent,
):
    n_row, n_col = lax.axis_size("row"), lax.axis_size("col")
    n_z = n_col // 2
    row_bits, z_bits = n_row.bit_length() - 1, n_z.bit_length() - 1
    total_nodes = TILE * n_row * n_col
    row, col = lax.axis_index("row"), lax.axis_index("col")
    core, z = col & 1, col >> 1

    def row_step(x, step):
        return exchange(x, n_row, n_col, (1 << step, 1 << (row_bits - 1 - step)), (0, 0))

    def z_step(x, step):
        return exchange(x, n_row, n_col, (0, 0), (1 << step, 1 << (z_bits - 1 - step)))

    def dot(a, b, dims):
        return lax.dot_general(a, b, (dims, ((), ())), preferred_element_type=FP)

    def place(q):
        return row ^ jnp.where(core == 0, q, reversed_bits(q, row_bits))

    here = [features]
    for q in range(1, n_row):
        here.append(exchange(features, n_row, n_col, (q, reversed_bits(q, row_bits)), (0, 0)))
    there = [swap_cores(x, n_row, n_col) for x in here]
    near, far = build(tile_vals, tile_row, tile_col, tile_count, n_row, n_col)
    far = swap_cores(far, n_row, n_col)
    onehot = (node_type[:, None] == jnp.arange(TYPES, dtype=jnp.int32)[None, :]).astype(FP)
    gains = jnp.dot(onehot, type_gain, precision=lax.Precision.HIGHEST)

    mid = near.shape[0] // 2
    here = jnp.concatenate(here + here, axis=0)
    part = product(near, here, mid)
    there = stacked(there, (part,))
    sent = rounded(part + dot(far[mid:], there, ((1,), (0,))))
    total = dot(near[:mid], here, ((1,), (0,))) + dot(far[:mid], there, ((1,), (0,)))
    for step in reversed(range(z_bits)):
        came = z_step(sent, step)
        if step:
            sent, total = added(total, came, True, ())
    aggregate, mine, away, activated, grad_hidden = node_values(total, came, gains, w_in, w_out, cotangent)

    met = swap_cores(away, n_row, n_col)
    node_rows = node_gradients(grad_hidden, w_in, aggregate, gains, cotangent, onehot.T)
    parts = 2
    sizes = (2 * TILE, 2 * TILE)
    lanes = [(sum(sizes[:i]), sizes[i]) for i in range(parts)]
    ahead, behind = range(n_row // 2, n_row), range(n_row // 2)
    first, node_rows = weight_blocks(mine, met, ahead, n_row, lanes[:1], BF, (node_rows,))
    sent = [first] + [weight_blocks(mine, met, ahead, n_row, [x], BF)[0] for x in lanes[1:]]
    *sums, mixed = weight_blocks(mine, met, behind, n_row, lanes, FP, (), (aggregate, activated, w_out))

    grad_rows, gain = node_rows[:TILE], node_rows[TILE:]
    for step in range(z_bits):
        came = z_step(jnp.concatenate([grad_rows, gain], axis=0), step)
        size = grad_rows.shape[0]
        grad_rows = jnp.concatenate([grad_rows, came[:size]], axis=0)
        gain = split(whole(gain) + whole(came[size:]))
    own = n_row * TILE
    came = swap_cores(rounded(dot(far[:, :own], grad_rows, ((0,), (0,)))), n_row, n_col)
    low = dot(near[:, :own], grad_rows, ((0,), (0,))) + came.astype(FP)
    marks = []
    for step in reversed(range(row_bits)):
        size = low.shape[0] // 2
        marks.append(jnp.concatenate([rounded(low[size:]), gain], axis=0))
        came = row_step(marks[-1], step)
        gain = split(whole(gain) + whole(came[size:]))
        low = low[:size] + came[:size].astype(FP)
    grad_x = low

    for step in reversed(range(row_bits)):
        for i in range(parts):
            mid = sums[i].shape[0] // 2
            came = row_step(sent[i], step)
            sums[i] = sums[i] + came.astype(FP)
            if step:
                sums[i], sent[i] = sums[i][:mid], rounded(sums[i][mid:])
    for step in range(z_bits):
        for i in range(parts):
            if step == 0:
                sent[i] = rounded(sums[i])
            came = z_step(sent[i], step)
            if step == 0 and i == parts - 1:
                sent[i] = added(sent[i], came, False, marks[:1])[0]
            else:
                sent[i] = rounded(sent[i].astype(FP) + came.astype(FP))
    for step in range(row_bits - 1):
        for i in range(parts):
            came = row_step(sent[i], step)
            if step == row_bits - 2:
                sent[i] = joined(sent[i], came, sent[:i] + (marks[-1:] if i == parts - 1 else []))
            else:
                sent[i] = jnp.concatenate([sent[i], came], axis=0)
    came = [row_step(x, row_bits - 1) for x in sent]

    factor = float(total_nodes) ** (-0.5)
    others = [swap_cores(x, n_row, n_col) for x in sent]
    gains = [gain, swap_cores(gain, n_row, n_col)]
    half = n_row // 2
    *weights, came[0] = write_weights(sent, others, [], [], 0, 0, n_row, factor, came[:1], [grad_x])
    others = [swap_cores(x, n_row, n_col) for x in came]
    for i in range(parts - 1):
        weights = write_weights(came[i : i + 1], others[i : i + 1], weights, [], half, lanes[i][0], n_row, factor)
    *weights, grad_gain = write_weights(came[-1:], others[-1:], weights, gains, half, lanes[-1][0], n_row, factor)
    grad_w_in, grad_w_out = weights
    return mixed, grad_x, grad_w_in, grad_w_out, grad_gain


def solution(mesh):
    return jax.shard_map(
        shards,
        mesh=mesh,
        in_specs=(
            P(("col", "row"), None),
            P("row", "col", None, None),
            P("row", "col"),
            P("row", "col"),
            P("row", "col"),
            P(("row", "col")),
            P(),
            P(),
            P(),
            P(("row", "col"), None),
        ),
        out_specs=(P(("row", "col"), None), P(("col", "row"), None), P(), P(), P()),
        check_vma=False,
    )
```

```python
import jax
import jax.numpy as jnp
import numpy as np
from jax import lax
from jax.experimental import pallas as pl
from jax.experimental.pallas import tpu as pltpu
from jax.sharding import PartitionSpec as P

F = 512
TYPES = 8
TILE = 128
BF = jnp.bfloat16
FP = jnp.float32
AXES = ("row", "col")


def reversed_bits(value, bits):
    out = 0
    for b in range(bits):
        out |= ((value >> b) & 1) << (bits - 1 - b)
    return out


def exchange(x, rows, cols, row_masks, z_masks):
    pairs = []
    for r in range(rows):
        for c in range(cols):
            core = c & 1
            pairs.append((r * cols + c, (r ^ row_masks[core]) * cols + (c ^ (2 * z_masks[core]))))
    return lax.ppermute(x, AXES, pairs)


def swap_cores(x, rows, cols):
    return lax.ppermute(x, AXES, [(i, i ^ 1) for i in range(rows * cols)])


def rounded(x):
    return lax.reduce_precision(x, 8, 7).astype(BF)


def split(x):
    high = lax.reduce_precision(x, 8, 7)
    return jnp.concatenate([high.astype(BF), rounded(x - high)], axis=0)


def whole(x):
    x = x.astype(FP)
    return x[:TYPES] + x[TYPES:]


def build(tile_vals, tile_row, tile_col, tile_count, n_row, n_col):
    slots = tile_vals.shape[1]
    n_z = n_col // 2
    wide, half = n_row * TILE, n_z * TILE
    chunk = 16
    rounds = slots // chunk

    def kernel(
        count_ref, rows_ref, cols_ref, vals_ref, near_ref, far_ref, total, held, row_ref, col_ref, sems
    ):
        places = [
            pltpu.make_async_copy(rows_ref, row_ref, sems.at[rounds]),
            pltpu.make_async_copy(cols_ref, col_ref, sems.at[rounds + 1]),
        ]
        for copy in places:
            copy.start()
        copies = []
        for i in range(rounds):
            at = pl.ds(i * chunk, chunk)
            copies.append(pltpu.make_async_copy(vals_ref.at[0, at], held.at[at], sems.at[i]))
            copies[i].start()
        row, col = lax.axis_index("row"), lax.axis_index("col")
        core, z = col & 1, col >> 1
        total[...] = jnp.zeros_like(total)
        count = count_ref[0, 0]
        for copy in places:
            copy.wait()

        def add(s, carry):
            r, c = row_ref[0, s], col_ref[0, s]
            total[r, c] = total[r, c] + held[s].astype(FP)
            return carry

        for i in range(rounds):
            copies[i].wait()
            lax.fori_loop(i * chunk, jnp.clip(count, i * chunk, (i + 1) * chunk), add, 0)

        for side, out in enumerate((near_ref, far_ref)):
            whose = core ^ side

            def emit(p, carry, out=out, whose=whose):
                r = 2 * (z ^ jnp.where(whose == 0, p, reversed_bits(p, n_z.bit_length() - 1))) + whose
                at = pl.ds(pl.multiple_of(p * TILE, TILE), TILE)
                for q in range(n_row):
                    value = total[r, row ^ jnp.where(core == 0, q, reversed_bits(q, n_row.bit_length() - 1))]
                    high = value.astype(BF)
                    out[at, q * TILE : (q + 1) * TILE] = high
                    out[at, wide + q * TILE : wide + (q + 1) * TILE] = (value - high.astype(FP)).astype(BF)
                return carry

            lax.fori_loop(0, n_z, emit, 0)

    dense = n_row * n_col * TILE * TILE
    result = jax.ShapeDtypeStruct((half, 2 * wide), BF)
    return pl.pallas_call(
        kernel,
        out_shape=(result, result),
        in_specs=[pl.BlockSpec(memory_space=pltpu.SMEM)] + [pl.BlockSpec(memory_space=pl.ANY)] * 3,
        scratch_shapes=[
            pltpu.VMEM((n_col, n_row, TILE, TILE), FP),
            pltpu.VMEM((slots, TILE, TILE), BF),
            pltpu.SMEM((1, slots), jnp.int32),
            pltpu.SMEM((1, slots), jnp.int32),
            pltpu.SemaphoreType.DMA((rounds + 2,)),
        ],
        compiler_params=pltpu.CompilerParams(vmem_limit_bytes=dense * 9 + 8 * 1024 * 1024),
        cost_estimate=pl.CostEstimate(
            flops=slots * TILE * TILE, bytes_accessed=slots * TILE * TILE * 2 + dense * 4, transcendentals=0
        ),
        name="build_dense",
    )(tile_count, *(pltpu.with_memory_space_constraint(x, pltpu.HBM) for x in (tile_row, tile_col, tile_vals)))


def write_weights(near, far, held, gains, first_place, first_lane, n_row, factor, through=(), after=()):
    parts = len(near)
    rows = near[0].shape[0]
    sizes = [x.shape[1] for x in near]
    width = sum(sizes)
    span = 2 * F // n_row
    places = rows // span
    per = F // span
    n_gain = len(gains) // 2

    def kernel(*refs):
        mine, there = refs[:parts], refs[parts : 2 * parts]
        outs = refs[2 * parts + len(held) + len(gains) + len(through) + len(after) :]
        in_ref, out_ref = outs[:2]
        wide_in, wide_out, sems = refs[-3:]
        core, row = lax.axis_index("col") & 1, lax.axis_index("row")

        def put(sources, ref, at):
            start = 0
            for x, size in zip(sources, sizes):
                ref[at, start : start + size] = x[at, :].astype(FP) * factor
                start += size

        copies = []
        if gains:
            one, two = (x[...].astype(FP) for x in refs[2 * parts + len(held) :][:2])
            small = refs[-4]
            small[...] = ((one[:TYPES] + one[TYPES:]) + (two[:TYPES] + two[TYPES:])) * factor
            copies.append(pltpu.make_async_copy(small, outs[2], sems.at[2 * places]))
            copies[-1].start()
        for j in range(places):
            q = first_place + j
            at = pl.ds(j * span, span)

            @pl.when(core == 0)
            def _(at=at):
                put(mine, wide_in, at)
                put(there, wide_out, at)

            @pl.when(core != 0)
            def _(at=at):
                put(there, wide_in, at)
                put(mine, wide_out, at)

            g = row ^ q
            to = in_ref.at[
                pl.ds(pl.multiple_of((g % per) * span, span), span),
                pl.ds(pl.multiple_of((g // per) * F + first_lane, TILE), width),
            ]
            copies.append(pltpu.make_async_copy(wide_in.at[at], to, sems.at[2 * j]))
            copies[-1].start()
            g = row ^ reversed_bits(q, n_row.bit_length() - 1)
            to = out_ref.at[pl.ds(pl.multiple_of(g * span, span), span), pl.ds(first_lane, width)]
            copies.append(pltpu.make_async_copy(wide_out.at[at], to, sems.at[2 * j + 1]))
            copies[-1].start()
        for copy in copies:
            copy.wait()

    vmem, hbm = pl.BlockSpec(memory_space=pltpu.VMEM), pl.BlockSpec(memory_space=pltpu.HBM)
    keep = pl.BlockSpec(memory_space=pl.ANY)
    before = 2 * parts + len(held) + len(gains)
    aliases = {2 * parts + i: i for i in range(len(held))}
    aliases.update({before + i: 2 + n_gain + i for i in range(len(through))})
    return pl.pallas_call(
        kernel,
        out_shape=(jax.ShapeDtypeStruct((F, 2 * F), FP), jax.ShapeDtypeStruct((2 * F, F), FP))
        + (jax.ShapeDtypeStruct((TYPES, F), FP),) * n_gain
        + tuple(jax.ShapeDtypeStruct(x.shape, x.dtype) for x in through),
        in_specs=[vmem] * (2 * parts) + [hbm] * len(held) + [vmem] * len(gains) + [keep] * (len(through) + len(after)),
        out_specs=(hbm, hbm) + (hbm,) * n_gain + (keep,) * len(through),
        input_output_aliases=aliases,
        scratch_shapes=[pltpu.VMEM((TYPES, F), FP)] * n_gain
        + [
            pltpu.VMEM((rows, width), FP),
            pltpu.VMEM((rows, width), FP),
            pltpu.SemaphoreType.DMA((2 * places + n_gain,)),
        ],
        compiler_params=pltpu.CompilerParams(vmem_limit_bytes=16 * 1024 * 1024),
        cost_estimate=pl.CostEstimate(flops=0, bytes_accessed=0, transcendentals=0),
        name="write_weights",
    )(*near, *far, *held, *gains, *through, *after)


def node_gradients(grad_hidden, w_in, aggregate, gains, cotangent, picked):
    rows = cotangent.shape[0]

    def kernel(gh_ref, w_ref, agg_ref, gains_ref, cot_ref, picked_ref, out_ref):
        aggregate = agg_ref[...]
        center = jnp.mean(aggregate, axis=-1, keepdims=True)
        spread = jnp.mean(jnp.square(aggregate - center), axis=-1, keepdims=True)
        inverse = lax.rsqrt(spread + 1e-05)
        normed = (aggregate - center) * inverse
        grad_scaled = lax.dot_general(
            gh_ref[...], w_ref[...], (((1,), (1,)), ((), ())), preferred_element_type=FP
        )
        grad_normed = grad_scaled * gains_ref[...]
        grad_agg = cot_ref[...].astype(FP) + inverse * (
            grad_normed
            - jnp.mean(grad_normed, axis=-1, keepdims=True)
            - normed * jnp.mean(grad_normed * normed, axis=-1, keepdims=True)
        )
        out_ref[:rows] = grad_agg.astype(BF)
        gain = jnp.dot(
            picked_ref[...], grad_scaled * normed, precision=lax.Precision.HIGHEST, preferred_element_type=FP
        )
        high = gain.astype(BF).astype(FP)
        out_ref[rows:] = jnp.concatenate([high, gain - high], axis=0).astype(BF)

    return pl.pallas_call(
        kernel,
        out_shape=jax.ShapeDtypeStruct((rows + 2 * TYPES, F), BF),
        in_specs=[pl.BlockSpec(memory_space=pltpu.VMEM)] * 6,
        out_specs=pl.BlockSpec(memory_space=pltpu.VMEM),
        compiler_params=pltpu.CompilerParams(vmem_limit_bytes=8 * 1024 * 1024),
        cost_estimate=pl.CostEstimate(flops=4 * rows * F * F, bytes_accessed=4 * F * F, transcendentals=rows),
        name="node_gradients",
    )(grad_hidden, w_in, aggregate, gains, cotangent, picked)


def weight_blocks(mine, met, places, n_row, lanes, dtype, through=(), mixing=()):
    span = 2 * F // n_row
    per = F // span
    rows = len(places) * span
    parts = len(lanes)
    extra = 1 if mixing else 0
    low, high = lanes[0][0], lanes[-1][0] + lanes[-1][1]

    def kernel(mine_ref, met_ref, *refs):
        outs = refs[len(through) + len(mixing) :][:parts]
        core, row = lax.axis_index("col") & 1, lax.axis_index("row")
        if mixing:
            aggregate, activated, w_out = refs[len(through) : len(through) + 3]
            held, sem = refs[-2:]
            branch = jnp.dot(activated[...], w_out[...], preferred_element_type=FP)
            held[...] = (aggregate[...] + branch).astype(BF)
            copy = pltpu.make_async_copy(held, refs[-3], sem)
            copy.start()

        def block(left, right):
            total = None
            for ref in (mine_ref, met_ref):
                term = lax.dot_general(
                    ref[:, left], ref[:, right], (((0,), (0,)), ((), ())), preferred_element_type=FP
                )
                total = term if total is None else total + term
            return total

        def put(j, value):
            for (start, size), out in zip(lanes, outs):
                out[j * span : (j + 1) * span, :] = value[:, start - low : start - low + size].astype(dtype)

        for j, q in enumerate(places):

            @pl.when(core == 0)
            def _(j=j, q=q):
                g = row ^ q
                left = pl.ds(pl.multiple_of((g % per) * span, span), span)
                right = pl.ds(pl.multiple_of(F + low + (g // per) * F, TILE), high - low)
                put(j, block(left, right))

            @pl.when(core != 0)
            def _(j=j, q=q):
                g = row ^ reversed_bits(q, n_row.bit_length() - 1)
                left = pl.ds(pl.multiple_of(F + g * span, span), span)
                put(j, block(left, slice(low, high)))

        if mixing:
            copy.wait()

    vmem, keep = pl.BlockSpec(memory_space=pltpu.VMEM), pl.BlockSpec(memory_space=pl.ANY)
    mixed = [jax.ShapeDtypeStruct(mixing[0].shape, BF)] if mixing else []
    return pl.pallas_call(
        kernel,
        out_shape=tuple(jax.ShapeDtypeStruct((rows, size), dtype) for _, size in lanes)
        + tuple(jax.ShapeDtypeStruct(x.shape, x.dtype) for x in (*through, *mixed)),
        in_specs=[vmem] * 2 + [keep] * len(through) + [vmem] * len(mixing),
        out_specs=(vmem,) * parts + (keep,) * len(through) + (pl.BlockSpec(memory_space=pltpu.HBM),) * extra,
        input_output_aliases={2 + i: parts + i for i in range(len(through))},
        scratch_shapes=[pltpu.VMEM(x.shape, BF) for x in mixed] + [pltpu.SemaphoreType.DMA] * extra,
        compiler_params=pltpu.CompilerParams(vmem_limit_bytes=8 * 1024 * 1024),
        cost_estimate=pl.CostEstimate(
            flops=4 * TILE * rows * (high - low), bytes_accessed=8 * TILE * F + 4 * rows * F, transcendentals=0
        ),
        name="weight_blocks",
    )(mine, met, *through, *mixing)


def small_call(kernel, name, outs, operands, after=()):
    n, m = len(operands), len(after)

    def body(*refs):
        kernel(*refs[:n], *refs[n + m :])

    moved = sum(x.size * x.dtype.itemsize for x in (*operands, *outs))
    vmem = pl.BlockSpec(memory_space=pltpu.VMEM)
    return pl.pallas_call(
        body,
        out_shape=tuple(outs),
        in_specs=[vmem] * n + [pl.BlockSpec(memory_space=pl.ANY)] * m,
        out_specs=(vmem,) * len(outs),
        compiler_params=pltpu.CompilerParams(vmem_limit_bytes=2 * moved + 4 * 1024 * 1024),
        cost_estimate=pl.CostEstimate(flops=0, bytes_accessed=0, transcendentals=0),
        name=name,
    )(*operands, *after)


def added(keep, came, halves, after):
    n, lanes = keep.shape
    half = n // 2

    def kernel(keep_ref, came_ref, *outs):
        if halves:
            outs[0][...] = (keep_ref[half:].astype(FP) + came_ref[half:].astype(FP)).astype(BF)
            outs[1][...] = keep_ref[:half].astype(FP) + came_ref[:half].astype(FP)
        else:
            outs[0][...] = (keep_ref[...].astype(FP) + came_ref[...].astype(FP)).astype(BF)

    if halves:
        outs = (jax.ShapeDtypeStruct((half, lanes), BF), jax.ShapeDtypeStruct((half, lanes), FP))
    else:
        outs = (jax.ShapeDtypeStruct((n, lanes), BF),)
    return small_call(kernel, "added", outs, (keep, came), after)


def node_values(keep, came, gains, w_in, w_out, cotangent):
    n = keep.shape[0]

    def kernel(keep_ref, came_ref, gains_ref, w_in_ref, w_out_ref, cot_ref, agg_ref, mine_ref, away_ref, act_ref, gh_ref):
        aggregate = keep_ref[...] + came_ref[...].astype(FP)
        agg_ref[...] = aggregate
        center = jnp.mean(aggregate, axis=-1, keepdims=True)
        spread = jnp.mean(jnp.square(aggregate - center), axis=-1, keepdims=True)
        inverse = lax.rsqrt(spread + 1e-05)
        scaled = ((aggregate - center) * inverse * gains_ref[...]).astype(BF)
        cot = cot_ref[...]
        grad_act = lax.dot_general(cot, w_out_ref[...], (((1,), (1,)), ((), ())), preferred_element_type=FP)
        hidden = jnp.dot(scaled, w_in_ref[...], preferred_element_type=FP)
        sigmoid_h = jax.nn.sigmoid(hidden)
        activated = (hidden * sigmoid_h).astype(BF)
        grad_hidden = (grad_act * sigmoid_h * (1.0 + hidden * (1.0 - sigmoid_h))).astype(BF)
        act_ref[...] = activated
        gh_ref[...] = grad_hidden

        def put(for_in, for_out):
            for_in[:, :F] = scaled
            for_in[:, F:] = grad_hidden
            for_out[:, :F] = cot
            for_out[:, F:] = activated

        first = lax.axis_index("col") & 1 == 0

        @pl.when(first)
        def _():
            put(mine_ref, away_ref)

        @pl.when(jnp.logical_not(first))
        def _():
            put(away_ref, mine_ref)

    outs = (jax.ShapeDtypeStruct((n, F), FP),) + tuple(jax.ShapeDtypeStruct((n, w * F), BF) for w in (3, 3, 2, 2))
    return small_call(kernel, "node_values", outs, (keep, came, gains, w_in, w_out, cotangent))


def joined(held, came, after):
    n, lanes = held.shape

    def kernel(held_ref, came_ref, out_ref):
        out_ref[:n] = held_ref[...]
        out_ref[n:] = came_ref[...]

    outs = (jax.ShapeDtypeStruct((2 * n, lanes), BF),)
    return small_call(kernel, "joined", outs, (held, came), after)[0]


def product(block, rows, first):
    n = block.shape[0] - first

    def kernel(block_ref, rows_ref, out_ref):
        out_ref[...] = jnp.dot(block_ref[first:], rows_ref[...], preferred_element_type=FP)

    return small_call(kernel, "product", (jax.ShapeDtypeStruct((n, F), FP),), (block, rows))[0]


def stacked(pieces, after):
    n = sum(x.shape[0] for x in pieces)

    def kernel(*refs):
        out_ref = refs[-1]
        at = 0
        for x in refs[:-1]:
            out_ref[at : at + x.shape[0]] = x[...]
            out_ref[n + at : n + at + x.shape[0]] = x[...]
            at += x.shape[0]

    return small_call(kernel, "stacked", (jax.ShapeDtypeStruct((2 * n, F), BF),), tuple(pieces), after)[0]


def shards(
    features,
    tile_vals,
    tile_row,
    tile_col,
    tile_count,
    node_type,
    type_gain,
    w_in,
    w_out,
    cotangent,
):
    n_row, n_col = lax.axis_size("row"), lax.axis_size("col")
    n_z = n_col // 2
    row_bits, z_bits = n_row.bit_length() - 1, n_z.bit_length() - 1
    total_nodes = TILE * n_row * n_col
    row, col = lax.axis_index("row"), lax.axis_index("col")
    core, z = col & 1, col >> 1

    def row_step(x, step):
        return exchange(x, n_row, n_col, (1 << step, 1 << (row_bits - 1 - step)), (0, 0))

    def z_step(x, step):
        return exchange(x, n_row, n_col, (0, 0), (1 << step, 1 << (z_bits - 1 - step)))

    def dot(a, b, dims):
        return lax.dot_general(a, b, (dims, ((), ())), preferred_element_type=FP)

    def place(q):
        return row ^ jnp.where(core == 0, q, reversed_bits(q, row_bits))

    here = [features]
    for q in range(1, n_row):
        here.append(exchange(features, n_row, n_col, (q, reversed_bits(q, row_bits)), (0, 0)))
    there = [swap_cores(x, n_row, n_col) for x in here]
    near, far = build(tile_vals, tile_row, tile_col, tile_count, n_row, n_col)
    far = swap_cores(far, n_row, n_col)
    onehot = (node_type[:, None] == jnp.arange(TYPES, dtype=jnp.int32)[None, :]).astype(FP)
    gains = jnp.dot(onehot, type_gain, precision=lax.Precision.HIGHEST)

    mid = near.shape[0] // 2
    here = jnp.concatenate(here + here, axis=0)
    part = product(near, here, mid)
    there = stacked(there, (part,))
    sent = rounded(part + dot(far[mid:], there, ((1,), (0,))))
    total = dot(near[:mid], here, ((1,), (0,))) + dot(far[:mid], there, ((1,), (0,)))
    for step in reversed(range(z_bits)):
        came = z_step(sent, step)
        if step:
            sent, total = added(total, came, True, ())
    aggregate, mine, away, activated, grad_hidden = node_values(total, came, gains, w_in, w_out, cotangent)

    met = swap_cores(away, n_row, n_col)
    node_rows = node_gradients(grad_hidden, w_in, aggregate, gains, cotangent, onehot.T)
    parts = 2
    sizes = (2 * TILE, 2 * TILE)
    lanes = [(sum(sizes[:i]), sizes[i]) for i in range(parts)]
    ahead, behind = range(n_row // 2, n_row), range(n_row // 2)
    first, node_rows = weight_blocks(mine, met, ahead, n_row, lanes[:1], BF, (node_rows,))
    sent = [first] + [weight_blocks(mine, met, ahead, n_row, [x], BF)[0] for x in lanes[1:]]
    *sums, mixed = weight_blocks(mine, met, behind, n_row, lanes, FP, (), (aggregate, activated, w_out))

    grad_rows, gain = node_rows[:TILE], node_rows[TILE:]
    for step in range(z_bits):
        came = z_step(jnp.concatenate([grad_rows, gain], axis=0), step)
        size = grad_rows.shape[0]
        grad_rows = jnp.concatenate([grad_rows, came[:size]], axis=0)
        gain = split(whole(gain) + whole(came[size:]))
    own = n_row * TILE
    came = swap_cores(rounded(dot(far[:, :own], grad_rows, ((0,), (0,)))), n_row, n_col)
    low = dot(near[:, :own], grad_rows, ((0,), (0,))) + came.astype(FP)
    marks = []
    for step in reversed(range(row_bits)):
        size = low.shape[0] // 2
        marks.append(jnp.concatenate([rounded(low[size:]), gain], axis=0))
        came = row_step(marks[-1], step)
        gain = split(whole(gain) + whole(came[size:]))
        low = low[:size] + came[:size].astype(FP)
    grad_x = low

    for step in reversed(range(row_bits)):
        for i in range(parts):
            mid = sums[i].shape[0] // 2
            came = row_step(sent[i], step)
            sums[i] = sums[i] + came.astype(FP)
            if step:
                sums[i], sent[i] = sums[i][:mid], rounded(sums[i][mid:])
    for step in range(z_bits):
        for i in range(parts):
            if step == 0:
                sent[i] = rounded(sums[i])
            came = z_step(sent[i], step)
            if step == 0 and i == parts - 1:
                sent[i] = added(sent[i], came, False, marks[:1])[0]
            else:
                sent[i] = rounded(sent[i].astype(FP) + came.astype(FP))
    for step in range(row_bits - 1):
        for i in range(parts):
            came = row_step(sent[i], step)
            if step == row_bits - 2:
                sent[i] = joined(sent[i], came, marks[-1:] if i == 0 else sent[:1])
            else:
                sent[i] = jnp.concatenate([sent[i], came], axis=0)
    came = [row_step(x, row_bits - 1) for x in sent]

    factor = float(total_nodes) ** (-0.5)
    others = [swap_cores(x, n_row, n_col) for x in sent]
    gains = [gain, swap_cores(gain, n_row, n_col)]
    half = n_row // 2
    *weights, grad_gain, came[0] = write_weights(sent, others, [], gains, 0, 0, n_row, factor, came[:1], [grad_x])
    others = [swap_cores(x, n_row, n_col) for x in came]
    for i in range(parts - 1):
        weights = write_weights(came[i : i + 1], others[i : i + 1], weights, [], half, lanes[i][0], n_row, factor)
    weights = write_weights(came[-1:], others[-1:], weights, [], half, lanes[-1][0], n_row, factor)
    grad_w_in, grad_w_out = weights
    return mixed, grad_x, grad_w_in, grad_w_out, grad_gain


def solution(mesh):
    return jax.shard_map(
        shards,
        mesh=mesh,
        in_specs=(
            P(("col", "row"), None),
            P("row", "col", None, None),
            P("row", "col"),
            P("row", "col"),
            P("row", "col"),
            P(("row", "col")),
            P(),
            P(),
            P(),
            P(("row", "col"), None),
        ),
        out_specs=(P(("row", "col"), None), P(("col", "row"), None), P(), P(), P()),
        check_vma=False,
    )
```

```python
import jax
import jax.numpy as jnp
import numpy as np
from jax import lax
from jax.experimental import pallas as pl
from jax.experimental.pallas import tpu as pltpu
from jax.sharding import PartitionSpec as P

F = 512
TYPES = 8
TILE = 128
BF = jnp.bfloat16
FP = jnp.float32
AXES = ("row", "col")


def reversed_bits(value, bits):
    out = 0
    for b in range(bits):
        out |= ((value >> b) & 1) << (bits - 1 - b)
    return out


def exchange(x, rows, cols, row_masks, z_masks):
    pairs = []
    for r in range(rows):
        for c in range(cols):
            core = c & 1
            pairs.append((r * cols + c, (r ^ row_masks[core]) * cols + (c ^ (2 * z_masks[core]))))
    return lax.ppermute(x, AXES, pairs)


def swap_cores(x, rows, cols):
    return lax.ppermute(x, AXES, [(i, i ^ 1) for i in range(rows * cols)])


def rounded(x):
    return lax.reduce_precision(x, 8, 7).astype(BF)


def split(x):
    high = lax.reduce_precision(x, 8, 7)
    return jnp.concatenate([high.astype(BF), rounded(x - high)], axis=0)


def whole(x):
    x = x.astype(FP)
    return x[:TYPES] + x[TYPES:]


def build(tile_vals, tile_row, tile_col, tile_count, n_row, n_col):
    slots = tile_vals.shape[1]
    n_z = n_col // 2
    wide, half = n_row * TILE, n_z * TILE
    chunk = 16
    rounds = slots // chunk

    def kernel(
        count_ref, rows_ref, cols_ref, vals_ref, near_ref, far_ref, total, held, row_ref, col_ref, sems
    ):
        places = [
            pltpu.make_async_copy(rows_ref, row_ref, sems.at[rounds]),
            pltpu.make_async_copy(cols_ref, col_ref, sems.at[rounds + 1]),
        ]
        for copy in places:
            copy.start()
        copies = []
        for i in range(rounds):
            at = pl.ds(i * chunk, chunk)
            copies.append(pltpu.make_async_copy(vals_ref.at[0, at], held.at[at], sems.at[i]))
            copies[i].start()
        row, col = lax.axis_index("row"), lax.axis_index("col")
        core, z = col & 1, col >> 1
        total[...] = jnp.zeros_like(total)
        count = count_ref[0, 0]
        for copy in places:
            copy.wait()

        def add(s, carry):
            r, c = row_ref[0, s], col_ref[0, s]
            total[r, c] = total[r, c] + held[s].astype(FP)
            return carry

        for i in range(rounds):
            copies[i].wait()
            lax.fori_loop(i * chunk, jnp.clip(count, i * chunk, (i + 1) * chunk), add, 0)

        for side, out in enumerate((near_ref, far_ref)):
            whose = core ^ side

            def emit(p, carry, out=out, whose=whose):
                r = 2 * (z ^ jnp.where(whose == 0, p, reversed_bits(p, n_z.bit_length() - 1))) + whose
                at = pl.ds(pl.multiple_of(p * TILE, TILE), TILE)
                for q in range(n_row):
                    value = total[r, row ^ jnp.where(core == 0, q, reversed_bits(q, n_row.bit_length() - 1))]
                    high = value.astype(BF)
                    out[at, q * TILE : (q + 1) * TILE] = high
                    out[at, wide + q * TILE : wide + (q + 1) * TILE] = (value - high.astype(FP)).astype(BF)
                return carry

            lax.fori_loop(0, n_z, emit, 0)

    dense = n_row * n_col * TILE * TILE
    result = jax.ShapeDtypeStruct((half, 2 * wide), BF)
    return pl.pallas_call(
        kernel,
        out_shape=(result, result),
        in_specs=[pl.BlockSpec(memory_space=pltpu.SMEM)] + [pl.BlockSpec(memory_space=pl.ANY)] * 3,
        scratch_shapes=[
            pltpu.VMEM((n_col, n_row, TILE, TILE), FP),
            pltpu.VMEM((slots, TILE, TILE), BF),
            pltpu.SMEM((1, slots), jnp.int32),
            pltpu.SMEM((1, slots), jnp.int32),
            pltpu.SemaphoreType.DMA((rounds + 2,)),
        ],
        compiler_params=pltpu.CompilerParams(vmem_limit_bytes=dense * 9 + 8 * 1024 * 1024),
        cost_estimate=pl.CostEstimate(
            flops=slots * TILE * TILE, bytes_accessed=slots * TILE * TILE * 2 + dense * 4, transcendentals=0
        ),
        name="build_dense",
    )(tile_count, *(pltpu.with_memory_space_constraint(x, pltpu.HBM) for x in (tile_row, tile_col, tile_vals)))


def write_weights(near, far, held, gains, first_place, first_lane, n_row, factor, through=(), after=()):
    parts = len(near)
    rows = near[0].shape[0]
    sizes = [x.shape[1] for x in near]
    width = sum(sizes)
    span = 2 * F // n_row
    places = rows // span
    per = F // span
    n_gain = len(gains) // 2

    def kernel(*refs):
        mine, there = refs[:parts], refs[parts : 2 * parts]
        outs = refs[2 * parts + len(held) + len(gains) + len(through) + len(after) :]
        in_ref, out_ref = outs[:2]
        wide_in, wide_out, sems = refs[-3:]
        core, row = lax.axis_index("col") & 1, lax.axis_index("row")

        def put(sources, ref, at):
            start = 0
            for x, size in zip(sources, sizes):
                ref[at, start : start + size] = x[at, :].astype(FP) * factor
                start += size

        copies = []
        if gains:
            one, two = (x[...].astype(FP) for x in refs[2 * parts + len(held) :][:2])
            small = refs[-4]
            small[...] = ((one[:TYPES] + one[TYPES:]) + (two[:TYPES] + two[TYPES:])) * factor
            copies.append(pltpu.make_async_copy(small, outs[2], sems.at[2 * places]))
            copies[-1].start()
        for j in range(places):
            q = first_place + j
            at = pl.ds(j * span, span)

            @pl.when(core == 0)
            def _(at=at):
                put(mine, wide_in, at)
                put(there, wide_out, at)

            @pl.when(core != 0)
            def _(at=at):
                put(there, wide_in, at)
                put(mine, wide_out, at)

            g = row ^ q
            to = in_ref.at[
                pl.ds(pl.multiple_of((g % per) * span, span), span),
                pl.ds(pl.multiple_of((g // per) * F + first_lane, TILE), width),
            ]
            copies.append(pltpu.make_async_copy(wide_in.at[at], to, sems.at[2 * j]))
            copies[-1].start()
            g = row ^ reversed_bits(q, n_row.bit_length() - 1)
            to = out_ref.at[pl.ds(pl.multiple_of(g * span, span), span), pl.ds(first_lane, width)]
            copies.append(pltpu.make_async_copy(wide_out.at[at], to, sems.at[2 * j + 1]))
            copies[-1].start()
        for copy in copies:
            copy.wait()

    vmem, hbm = pl.BlockSpec(memory_space=pltpu.VMEM), pl.BlockSpec(memory_space=pltpu.HBM)
    keep = pl.BlockSpec(memory_space=pl.ANY)
    before = 2 * parts + len(held) + len(gains)
    aliases = {2 * parts + i: i for i in range(len(held))}
    aliases.update({before + i: 2 + n_gain + i for i in range(len(through))})
    return pl.pallas_call(
        kernel,
        out_shape=(jax.ShapeDtypeStruct((F, 2 * F), FP), jax.ShapeDtypeStruct((2 * F, F), FP))
        + (jax.ShapeDtypeStruct((TYPES, F), FP),) * n_gain
        + tuple(jax.ShapeDtypeStruct(x.shape, x.dtype) for x in through),
        in_specs=[vmem] * (2 * parts) + [hbm] * len(held) + [vmem] * len(gains) + [keep] * (len(through) + len(after)),
        out_specs=(hbm, hbm) + (hbm,) * n_gain + (keep,) * len(through),
        input_output_aliases=aliases,
        scratch_shapes=[pltpu.VMEM((TYPES, F), FP)] * n_gain
        + [
            pltpu.VMEM((rows, width), FP),
            pltpu.VMEM((rows, width), FP),
            pltpu.SemaphoreType.DMA((2 * places + n_gain,)),
        ],
        compiler_params=pltpu.CompilerParams(vmem_limit_bytes=16 * 1024 * 1024),
        cost_estimate=pl.CostEstimate(flops=0, bytes_accessed=0, transcendentals=0),
        name="write_weights",
    )(*near, *far, *held, *gains, *through, *after)


def node_gradients(grad_hidden, w_in, aggregate, gains, cotangent, picked):
    rows = cotangent.shape[0]

    def kernel(gh_ref, w_ref, agg_ref, gains_ref, cot_ref, picked_ref, out_ref):
        aggregate = agg_ref[...]
        center = jnp.mean(aggregate, axis=-1, keepdims=True)
        spread = jnp.mean(jnp.square(aggregate - center), axis=-1, keepdims=True)
        inverse = lax.rsqrt(spread + 1e-05)
        normed = (aggregate - center) * inverse
        grad_scaled = lax.dot_general(
            gh_ref[...], w_ref[...], (((1,), (1,)), ((), ())), preferred_element_type=FP
        )
        grad_normed = grad_scaled * gains_ref[...]
        grad_agg = cot_ref[...].astype(FP) + inverse * (
            grad_normed
            - jnp.mean(grad_normed, axis=-1, keepdims=True)
            - normed * jnp.mean(grad_normed * normed, axis=-1, keepdims=True)
        )
        out_ref[:rows] = grad_agg.astype(BF)
        gain = jnp.dot(
            picked_ref[...], grad_scaled * normed, precision=lax.Precision.HIGHEST, preferred_element_type=FP
        )
        high = gain.astype(BF).astype(FP)
        out_ref[rows:] = jnp.concatenate([high, gain - high], axis=0).astype(BF)

    return pl.pallas_call(
        kernel,
        out_shape=jax.ShapeDtypeStruct((rows + 2 * TYPES, F), BF),
        in_specs=[pl.BlockSpec(memory_space=pltpu.VMEM)] * 6,
        out_specs=pl.BlockSpec(memory_space=pltpu.VMEM),
        compiler_params=pltpu.CompilerParams(vmem_limit_bytes=8 * 1024 * 1024),
        cost_estimate=pl.CostEstimate(flops=4 * rows * F * F, bytes_accessed=4 * F * F, transcendentals=rows),
        name="node_gradients",
    )(grad_hidden, w_in, aggregate, gains, cotangent, picked)


def weight_blocks(mine, met, places, n_row, lanes, dtype, through=(), mixing=()):
    span = 2 * F // n_row
    per = F // span
    rows = len(places) * span
    parts = len(lanes)
    extra = 1 if mixing else 0
    low, high = lanes[0][0], lanes[-1][0] + lanes[-1][1]

    def kernel(mine_ref, met_ref, *refs):
        outs = refs[len(through) + len(mixing) :][:parts]
        core, row = lax.axis_index("col") & 1, lax.axis_index("row")
        if mixing:
            aggregate, activated, w_out = refs[len(through) : len(through) + 3]
            held, sem = refs[-2:]
            branch = jnp.dot(activated[...], w_out[...], preferred_element_type=FP)
            held[...] = (aggregate[...] + branch).astype(BF)
            copy = pltpu.make_async_copy(held, refs[-3], sem)
            copy.start()

        def block(left, right):
            total = None
            for ref in (mine_ref, met_ref):
                term = lax.dot_general(
                    ref[:, left], ref[:, right], (((0,), (0,)), ((), ())), preferred_element_type=FP
                )
                total = term if total is None else total + term
            return total

        def put(j, value):
            for (start, size), out in zip(lanes, outs):
                out[j * span : (j + 1) * span, :] = value[:, start - low : start - low + size].astype(dtype)

        for j, q in enumerate(places):

            @pl.when(core == 0)
            def _(j=j, q=q):
                g = row ^ q
                left = pl.ds(pl.multiple_of((g % per) * span, span), span)
                right = pl.ds(pl.multiple_of(F + low + (g // per) * F, TILE), high - low)
                put(j, block(left, right))

            @pl.when(core != 0)
            def _(j=j, q=q):
                g = row ^ reversed_bits(q, n_row.bit_length() - 1)
                left = pl.ds(pl.multiple_of(F + g * span, span), span)
                put(j, block(left, slice(low, high)))

        if mixing:
            copy.wait()

    vmem, keep = pl.BlockSpec(memory_space=pltpu.VMEM), pl.BlockSpec(memory_space=pl.ANY)
    mixed = [jax.ShapeDtypeStruct(mixing[0].shape, BF)] if mixing else []
    return pl.pallas_call(
        kernel,
        out_shape=tuple(jax.ShapeDtypeStruct((rows, size), dtype) for _, size in lanes)
        + tuple(jax.ShapeDtypeStruct(x.shape, x.dtype) for x in (*through, *mixed)),
        in_specs=[vmem] * 2 + [keep] * len(through) + [vmem] * len(mixing),
        out_specs=(vmem,) * parts + (keep,) * len(through) + (pl.BlockSpec(memory_space=pltpu.HBM),) * extra,
        input_output_aliases={2 + i: parts + i for i in range(len(through))},
        scratch_shapes=[pltpu.VMEM(x.shape, BF) for x in mixed] + [pltpu.SemaphoreType.DMA] * extra,
        compiler_params=pltpu.CompilerParams(vmem_limit_bytes=8 * 1024 * 1024),
        cost_estimate=pl.CostEstimate(
            flops=4 * TILE * rows * (high - low), bytes_accessed=8 * TILE * F + 4 * rows * F, transcendentals=0
        ),
        name="weight_blocks",
    )(mine, met, *through, *mixing)


def small_call(kernel, name, outs, operands, after=()):
    n, m = len(operands), len(after)

    def body(*refs):
        kernel(*refs[:n], *refs[n + m :])

    moved = sum(x.size * x.dtype.itemsize for x in (*operands, *outs))
    vmem = pl.BlockSpec(memory_space=pltpu.VMEM)
    return pl.pallas_call(
        body,
        out_shape=tuple(outs),
        in_specs=[vmem] * n + [pl.BlockSpec(memory_space=pl.ANY)] * m,
        out_specs=(vmem,) * len(outs),
        compiler_params=pltpu.CompilerParams(vmem_limit_bytes=2 * moved + 4 * 1024 * 1024),
        cost_estimate=pl.CostEstimate(flops=0, bytes_accessed=0, transcendentals=0),
        name=name,
    )(*operands, *after)


def added(keep, came, halves, after):
    n, lanes = keep.shape
    half = n // 2

    def kernel(keep_ref, came_ref, *outs):
        if halves:
            outs[0][...] = (keep_ref[half:].astype(FP) + came_ref[half:].astype(FP)).astype(BF)
            outs[1][...] = keep_ref[:half].astype(FP) + came_ref[:half].astype(FP)
        else:
            outs[0][...] = (keep_ref[...].astype(FP) + came_ref[...].astype(FP)).astype(BF)

    if halves:
        outs = (jax.ShapeDtypeStruct((half, lanes), BF), jax.ShapeDtypeStruct((half, lanes), FP))
    else:
        outs = (jax.ShapeDtypeStruct((n, lanes), BF),)
    return small_call(kernel, "added", outs, (keep, came), after)


def node_values(keep, came, gains, w_in, w_out, cotangent):
    n = keep.shape[0]

    def kernel(keep_ref, came_ref, gains_ref, w_in_ref, w_out_ref, cot_ref, agg_ref, mine_ref, away_ref, act_ref, gh_ref):
        aggregate = keep_ref[...] + came_ref[...].astype(FP)
        agg_ref[...] = aggregate
        center = jnp.mean(aggregate, axis=-1, keepdims=True)
        spread = jnp.mean(jnp.square(aggregate - center), axis=-1, keepdims=True)
        inverse = lax.rsqrt(spread + 1e-05)
        scaled = ((aggregate - center) * inverse * gains_ref[...]).astype(BF)
        cot = cot_ref[...]
        grad_act = lax.dot_general(cot, w_out_ref[...], (((1,), (1,)), ((), ())), preferred_element_type=FP)
        hidden = jnp.dot(scaled, w_in_ref[...], preferred_element_type=FP)
        sigmoid_h = jax.nn.sigmoid(hidden)
        activated = (hidden * sigmoid_h).astype(BF)
        grad_hidden = (grad_act * sigmoid_h * (1.0 + hidden * (1.0 - sigmoid_h))).astype(BF)
        act_ref[...] = activated
        gh_ref[...] = grad_hidden

        def put(for_in, for_out):
            for_in[:, :F] = scaled
            for_in[:, F:] = grad_hidden
            for_out[:, :F] = cot
            for_out[:, F:] = activated

        first = lax.axis_index("col") & 1 == 0

        @pl.when(first)
        def _():
            put(mine_ref, away_ref)

        @pl.when(jnp.logical_not(first))
        def _():
            put(away_ref, mine_ref)

    outs = (jax.ShapeDtypeStruct((n, F), FP),) + tuple(jax.ShapeDtypeStruct((n, w * F), BF) for w in (3, 3, 2, 2))
    return small_call(kernel, "node_values", outs, (keep, came, gains, w_in, w_out, cotangent))


def joined(held, came, after):
    n, lanes = held.shape

    def kernel(held_ref, came_ref, out_ref):
        out_ref[:n] = held_ref[...]
        out_ref[n:] = came_ref[...]

    outs = (jax.ShapeDtypeStruct((2 * n, lanes), BF),)
    return small_call(kernel, "joined", outs, (held, came), after)[0]


def product(block, rows, first):
    n = block.shape[0] - first

    def kernel(block_ref, rows_ref, out_ref):
        out_ref[...] = jnp.dot(block_ref[first:], rows_ref[...], preferred_element_type=FP)

    return small_call(kernel, "product", (jax.ShapeDtypeStruct((n, F), FP),), (block, rows))[0]


def stacked(pieces, after):
    n = sum(x.shape[0] for x in pieces)

    def kernel(*refs):
        out_ref = refs[-1]
        at = 0
        for x in refs[:-1]:
            out_ref[at : at + x.shape[0]] = x[...]
            out_ref[n + at : n + at + x.shape[0]] = x[...]
            at += x.shape[0]

    return small_call(kernel, "stacked", (jax.ShapeDtypeStruct((2 * n, F), BF),), tuple(pieces), after)[0]


def shards(
    features,
    tile_vals,
    tile_row,
    tile_col,
    tile_count,
    node_type,
    type_gain,
    w_in,
    w_out,
    cotangent,
):
    n_row, n_col = lax.axis_size("row"), lax.axis_size("col")
    n_z = n_col // 2
    row_bits, z_bits = n_row.bit_length() - 1, n_z.bit_length() - 1
    total_nodes = TILE * n_row * n_col
    row, col = lax.axis_index("row"), lax.axis_index("col")
    core, z = col & 1, col >> 1

    def row_step(x, step):
        return exchange(x, n_row, n_col, (1 << step, 1 << (row_bits - 1 - step)), (0, 0))

    def z_step(x, step):
        return exchange(x, n_row, n_col, (0, 0), (1 << step, 1 << (z_bits - 1 - step)))

    def dot(a, b, dims):
        return lax.dot_general(a, b, (dims, ((), ())), preferred_element_type=FP)

    def place(q):
        return row ^ jnp.where(core == 0, q, reversed_bits(q, row_bits))

    here = [features]
    for q in range(1, n_row):
        here.append(exchange(features, n_row, n_col, (q, reversed_bits(q, row_bits)), (0, 0)))
    there = [swap_cores(x, n_row, n_col) for x in here]
    near, far = build(tile_vals, tile_row, tile_col, tile_count, n_row, n_col)
    far = swap_cores(far, n_row, n_col)
    onehot = (node_type[:, None] == jnp.arange(TYPES, dtype=jnp.int32)[None, :]).astype(FP)
    gains = jnp.dot(onehot, type_gain, precision=lax.Precision.HIGHEST)

    mid = near.shape[0] // 2
    here = jnp.concatenate(here + here, axis=0)
    part = product(near, here, mid)
    there = stacked(there, (part,))
    sent = rounded(part + dot(far[mid:], there, ((1,), (0,))))
    total = dot(near[:mid], here, ((1,), (0,))) + dot(far[:mid], there, ((1,), (0,)))
    for step in reversed(range(z_bits)):
        came = z_step(sent, step)
        if step:
            sent, total = added(total, came, True, ())
    aggregate, mine, away, activated, grad_hidden = node_values(total, came, gains, w_in, w_out, cotangent)

    met = swap_cores(away, n_row, n_col)
    node_rows = node_gradients(grad_hidden, w_in, aggregate, gains, cotangent, onehot.T)
    parts = 2
    sizes = (2 * TILE, 2 * TILE)
    lanes = [(sum(sizes[:i]), sizes[i]) for i in range(parts)]
    ahead, behind = range(n_row // 2, n_row), range(n_row // 2)
    first, node_rows = weight_blocks(mine, met, ahead, n_row, lanes[:1], BF, (node_rows,))
    sent = [first] + [weight_blocks(mine, met, ahead, n_row, [x], BF)[0] for x in lanes[1:]]
    *sums, mixed = weight_blocks(mine, met, behind, n_row, lanes, FP, (), (aggregate, activated, w_out))

    grad_rows, gain = node_rows[:TILE], node_rows[TILE:]
    for step in range(z_bits):
        came = z_step(jnp.concatenate([grad_rows, gain], axis=0), step)
        size = grad_rows.shape[0]
        grad_rows = jnp.concatenate([grad_rows, came[:size]], axis=0)
        gain = split(whole(gain) + whole(came[size:]))
    own = n_row * TILE
    came = swap_cores(rounded(dot(far[:, :own], grad_rows, ((0,), (0,)))), n_row, n_col)
    low = dot(near[:, :own], grad_rows, ((0,), (0,))) + came.astype(FP)
    marks = []
    tiles = [low[q * TILE : (q + 1) * TILE] for q in range(n_row)]
    for step in range(row_bits):
        marks.append(jnp.concatenate([rounded(x) for x in tiles[1::2]] + [gain], axis=0))
        came = row_step(marks[-1], step)
        tiles = [x + came[i * TILE : (i + 1) * TILE].astype(FP) for i, x in enumerate(tiles[0::2])]
        gain = split(whole(gain) + whole(came[len(tiles) * TILE :]))
    grad_x = tiles[0]

    for step in reversed(range(row_bits)):
        for i in range(parts):
            mid = sums[i].shape[0] // 2
            came = row_step(sent[i], step)
            sums[i] = sums[i] + came.astype(FP)
            if step:
                sums[i], sent[i] = sums[i][:mid], rounded(sums[i][mid:])
    for step in range(z_bits):
        for i in range(parts):
            if step == 0:
                sent[i] = rounded(sums[i])
            came = z_step(sent[i], step)
            if step == 0 and i == parts - 1:
                sent[i] = added(sent[i], came, False, marks[:1])[0]
            else:
                sent[i] = rounded(sent[i].astype(FP) + came.astype(FP))
    for step in range(row_bits - 1):
        for i in range(parts):
            came = row_step(sent[i], step)
            if step == row_bits - 2:
                sent[i] = joined(sent[i], came, marks[-1:] if i == 0 else sent[:1])
            else:
                sent[i] = jnp.concatenate([sent[i], came], axis=0)
    came = [row_step(x, row_bits - 1) for x in sent]

    factor = float(total_nodes) ** (-0.5)
    others = [swap_cores(x, n_row, n_col) for x in sent]
    gains = [gain, swap_cores(gain, n_row, n_col)]
    half = n_row // 2
    *weights, grad_gain, came[0] = write_weights(sent, others, [], gains, 0, 0, n_row, factor, came[:1], [grad_x])
    others = [swap_cores(x, n_row, n_col) for x in came]
    for i in range(parts - 1):
        weights = write_weights(came[i : i + 1], others[i : i + 1], weights, [], half, lanes[i][0], n_row, factor)
    weights = write_weights(came[-1:], others[-1:], weights, [], half, lanes[-1][0], n_row, factor)
    grad_w_in, grad_w_out = weights
    return mixed, grad_x, grad_w_in, grad_w_out, grad_gain


def solution(mesh):
    return jax.shard_map(
        shards,
        mesh=mesh,
        in_specs=(
            P(("col", "row"), None),
            P("row", "col", None, None),
            P("row", "col"),
            P("row", "col"),
            P("row", "col"),
            P(("row", "col")),
            P(),
            P(),
            P(),
            P(("row", "col"), None),
        ),
        out_specs=(P(("row", "col"), None), P(("col", "row"), None), P(), P(), P()),
        check_vma=False,
    )
```

```python
import jax
import jax.numpy as jnp
import numpy as np
from jax import lax
from jax.experimental import pallas as pl
from jax.experimental.pallas import tpu as pltpu
from jax.sharding import PartitionSpec as P

F = 512
TYPES = 8
TILE = 128
BF = jnp.bfloat16
FP = jnp.float32
AXES = ("row", "col")


def reversed_bits(value, bits):
    out = 0
    for b in range(bits):
        out |= ((value >> b) & 1) << (bits - 1 - b)
    return out


def exchange(x, rows, cols, row_masks, z_masks):
    pairs = []
    for r in range(rows):
        for c in range(cols):
            core = c & 1
            pairs.append((r * cols + c, (r ^ row_masks[core]) * cols + (c ^ (2 * z_masks[core]))))
    return lax.ppermute(x, AXES, pairs)


def swap_cores(x, rows, cols):
    return lax.ppermute(x, AXES, [(i, i ^ 1) for i in range(rows * cols)])


def rounded(x):
    return lax.reduce_precision(x, 8, 7).astype(BF)


def split(x):
    high = lax.reduce_precision(x, 8, 7)
    return jnp.concatenate([high.astype(BF), rounded(x - high)], axis=0)


def whole(x):
    x = x.astype(FP)
    return x[:TYPES] + x[TYPES:]


def build(tile_vals, tile_row, tile_col, tile_count, n_row, n_col):
    slots = tile_vals.shape[1]
    n_z = n_col // 2
    wide, half = n_row * TILE, n_z * TILE
    chunk = 16
    rounds = slots // chunk

    def kernel(
        count_ref, rows_ref, cols_ref, vals_ref, near_ref, far_ref, total, held, row_ref, col_ref, sems
    ):
        places = [
            pltpu.make_async_copy(rows_ref, row_ref, sems.at[rounds]),
            pltpu.make_async_copy(cols_ref, col_ref, sems.at[rounds + 1]),
        ]
        for copy in places:
            copy.start()
        copies = []
        for i in range(rounds):
            at = pl.ds(i * chunk, chunk)
            copies.append(pltpu.make_async_copy(vals_ref.at[0, at], held.at[at], sems.at[i]))
            copies[i].start()
        row, col = lax.axis_index("row"), lax.axis_index("col")
        core, z = col & 1, col >> 1
        total[...] = jnp.zeros_like(total)
        count = count_ref[0, 0]
        for copy in places:
            copy.wait()

        def add(s, carry):
            r, c = row_ref[0, s], col_ref[0, s]
            total[r, c] = total[r, c] + held[s].astype(FP)
            return carry

        for i in range(rounds):
            copies[i].wait()
            lax.fori_loop(i * chunk, jnp.clip(count, i * chunk, (i + 1) * chunk), add, 0)

        for side, out in enumerate((near_ref, far_ref)):
            whose = core ^ side

            def emit(p, carry, out=out, whose=whose):
                r = 2 * (z ^ jnp.where(whose == 0, p, reversed_bits(p, n_z.bit_length() - 1))) + whose
                at = pl.ds(pl.multiple_of(p * TILE, TILE), TILE)
                for q in range(n_row):
                    value = total[r, row ^ jnp.where(core == 0, q, reversed_bits(q, n_row.bit_length() - 1))]
                    high = value.astype(BF)
                    out[at, q * TILE : (q + 1) * TILE] = high
                    out[at, wide + q * TILE : wide + (q + 1) * TILE] = (value - high.astype(FP)).astype(BF)
                return carry

            lax.fori_loop(0, n_z, emit, 0)

    dense = n_row * n_col * TILE * TILE
    result = jax.ShapeDtypeStruct((half, 2 * wide), BF)
    return pl.pallas_call(
        kernel,
        out_shape=(result, result),
        in_specs=[pl.BlockSpec(memory_space=pltpu.SMEM)] + [pl.BlockSpec(memory_space=pl.ANY)] * 3,
        scratch_shapes=[
            pltpu.VMEM((n_col, n_row, TILE, TILE), FP),
            pltpu.VMEM((slots, TILE, TILE), BF),
            pltpu.SMEM((1, slots), jnp.int32),
            pltpu.SMEM((1, slots), jnp.int32),
            pltpu.SemaphoreType.DMA((rounds + 2,)),
        ],
        compiler_params=pltpu.CompilerParams(vmem_limit_bytes=dense * 9 + 8 * 1024 * 1024),
        cost_estimate=pl.CostEstimate(
            flops=slots * TILE * TILE, bytes_accessed=slots * TILE * TILE * 2 + dense * 4, transcendentals=0
        ),
        name="build_dense",
    )(tile_count, *(pltpu.with_memory_space_constraint(x, pltpu.HBM) for x in (tile_row, tile_col, tile_vals)))


def write_weights(near, far, held, gains, first_place, first_lane, n_row, factor, through=(), after=()):
    parts = len(near)
    rows = near[0].shape[0]
    sizes = [x.shape[1] for x in near]
    width = sum(sizes)
    span = 2 * F // n_row
    places = rows // span
    per = F // span
    n_gain = len(gains) // 2

    def kernel(*refs):
        mine, there = refs[:parts], refs[parts : 2 * parts]
        outs = refs[2 * parts + len(held) + len(gains) + len(through) + len(after) :]
        in_ref, out_ref = outs[:2]
        wide_in, wide_out, sems = refs[-3:]
        core, row = lax.axis_index("col") & 1, lax.axis_index("row")

        def put(sources, ref, at):
            start = 0
            for x, size in zip(sources, sizes):
                ref[at, start : start + size] = x[at, :].astype(FP) * factor
                start += size

        copies = []
        if gains:
            one, two = (x[...].astype(FP) for x in refs[2 * parts + len(held) :][:2])
            small = refs[-4]
            small[...] = ((one[:TYPES] + one[TYPES:]) + (two[:TYPES] + two[TYPES:])) * factor
            copies.append(pltpu.make_async_copy(small, outs[2], sems.at[2 * places]))
            copies[-1].start()
        for j in range(places):
            q = first_place + j
            at = pl.ds(j * span, span)

            @pl.when(core == 0)
            def _(at=at):
                put(mine, wide_in, at)
                put(there, wide_out, at)

            @pl.when(core != 0)
            def _(at=at):
                put(there, wide_in, at)
                put(mine, wide_out, at)

            g = row ^ q
            to = in_ref.at[
                pl.ds(pl.multiple_of((g % per) * span, span), span),
                pl.ds(pl.multiple_of((g // per) * F + first_lane, TILE), width),
            ]
            copies.append(pltpu.make_async_copy(wide_in.at[at], to, sems.at[2 * j]))
            copies[-1].start()
            g = row ^ reversed_bits(q, n_row.bit_length() - 1)
            to = out_ref.at[pl.ds(pl.multiple_of(g * span, span), span), pl.ds(first_lane, width)]
            copies.append(pltpu.make_async_copy(wide_out.at[at], to, sems.at[2 * j + 1]))
            copies[-1].start()
        for copy in copies:
            copy.wait()

    vmem, hbm = pl.BlockSpec(memory_space=pltpu.VMEM), pl.BlockSpec(memory_space=pltpu.HBM)
    keep = pl.BlockSpec(memory_space=pl.ANY)
    before = 2 * parts + len(held) + len(gains)
    aliases = {2 * parts + i: i for i in range(len(held))}
    aliases.update({before + i: 2 + n_gain + i for i in range(len(through))})
    return pl.pallas_call(
        kernel,
        out_shape=(jax.ShapeDtypeStruct((F, 2 * F), FP), jax.ShapeDtypeStruct((2 * F, F), FP))
        + (jax.ShapeDtypeStruct((TYPES, F), FP),) * n_gain
        + tuple(jax.ShapeDtypeStruct(x.shape, x.dtype) for x in through),
        in_specs=[vmem] * (2 * parts) + [hbm] * len(held) + [vmem] * len(gains) + [keep] * (len(through) + len(after)),
        out_specs=(hbm, hbm) + (hbm,) * n_gain + (keep,) * len(through),
        input_output_aliases=aliases,
        scratch_shapes=[pltpu.VMEM((TYPES, F), FP)] * n_gain
        + [
            pltpu.VMEM((rows, width), FP),
            pltpu.VMEM((rows, width), FP),
            pltpu.SemaphoreType.DMA((2 * places + n_gain,)),
        ],
        compiler_params=pltpu.CompilerParams(vmem_limit_bytes=16 * 1024 * 1024),
        cost_estimate=pl.CostEstimate(flops=0, bytes_accessed=0, transcendentals=0),
        name="write_weights",
    )(*near, *far, *held, *gains, *through, *after)


def node_gradients(grad_hidden, w_in, aggregate, gains, cotangent, picked):
    rows = cotangent.shape[0]

    def kernel(gh_ref, w_ref, agg_ref, gains_ref, cot_ref, picked_ref, out_ref):
        aggregate = agg_ref[...]
        center = jnp.mean(aggregate, axis=-1, keepdims=True)
        spread = jnp.mean(jnp.square(aggregate - center), axis=-1, keepdims=True)
        inverse = lax.rsqrt(spread + 1e-05)
        normed = (aggregate - center) * inverse
        grad_scaled = lax.dot_general(
            gh_ref[...], w_ref[...], (((1,), (1,)), ((), ())), preferred_element_type=FP
        )
        grad_normed = grad_scaled * gains_ref[...]
        grad_agg = cot_ref[...].astype(FP) + inverse * (
            grad_normed
            - jnp.mean(grad_normed, axis=-1, keepdims=True)
            - normed * jnp.mean(grad_normed * normed, axis=-1, keepdims=True)
        )
        out_ref[:rows] = grad_agg.astype(BF)
        gain = jnp.dot(
            picked_ref[...], grad_scaled * normed, precision=lax.Precision.HIGHEST, preferred_element_type=FP
        )
        high = gain.astype(BF).astype(FP)
        out_ref[rows:] = jnp.concatenate([high, gain - high], axis=0).astype(BF)

    return pl.pallas_call(
        kernel,
        out_shape=jax.ShapeDtypeStruct((rows + 2 * TYPES, F), BF),
        in_specs=[pl.BlockSpec(memory_space=pltpu.VMEM)] * 6,
        out_specs=pl.BlockSpec(memory_space=pltpu.VMEM),
        compiler_params=pltpu.CompilerParams(vmem_limit_bytes=8 * 1024 * 1024),
        cost_estimate=pl.CostEstimate(flops=4 * rows * F * F, bytes_accessed=4 * F * F, transcendentals=rows),
        name="node_gradients",
    )(grad_hidden, w_in, aggregate, gains, cotangent, picked)


def weight_blocks(mine, met, places, n_row, lanes, dtype, through=(), mixing=()):
    span = 2 * F // n_row
    per = F // span
    rows = len(places) * span
    parts = len(lanes)
    extra = 1 if mixing else 0
    low, high = lanes[0][0], lanes[-1][0] + lanes[-1][1]

    def kernel(mine_ref, met_ref, *refs):
        outs = refs[len(through) + len(mixing) :][:parts]
        core, row = lax.axis_index("col") & 1, lax.axis_index("row")
        if mixing:
            aggregate, activated, w_out = refs[len(through) : len(through) + 3]
            held, sem = refs[-2:]
            branch = jnp.dot(activated[...], w_out[...], preferred_element_type=FP)
            held[...] = (aggregate[...] + branch).astype(BF)
            copy = pltpu.make_async_copy(held, refs[-3], sem)
            copy.start()

        def block(left, right):
            total = None
            for ref in (mine_ref, met_ref):
                term = lax.dot_general(
                    ref[:, left], ref[:, right], (((0,), (0,)), ((), ())), preferred_element_type=FP
                )
                total = term if total is None else total + term
            return total

        def put(j, value):
            for (start, size), out in zip(lanes, outs):
                out[j * span : (j + 1) * span, :] = value[:, start - low : start - low + size].astype(dtype)

        for j, q in enumerate(places):

            @pl.when(core == 0)
            def _(j=j, q=q):
                g = row ^ q
                left = pl.ds(pl.multiple_of((g % per) * span, span), span)
                right = pl.ds(pl.multiple_of(F + low + (g // per) * F, TILE), high - low)
                put(j, block(left, right))

            @pl.when(core != 0)
            def _(j=j, q=q):
                g = row ^ reversed_bits(q, n_row.bit_length() - 1)
                left = pl.ds(pl.multiple_of(F + g * span, span), span)
                put(j, block(left, slice(low, high)))

        if mixing:
            copy.wait()

    vmem, keep = pl.BlockSpec(memory_space=pltpu.VMEM), pl.BlockSpec(memory_space=pl.ANY)
    mixed = [jax.ShapeDtypeStruct(mixing[0].shape, BF)] if mixing else []
    return pl.pallas_call(
        kernel,
        out_shape=tuple(jax.ShapeDtypeStruct((rows, size), dtype) for _, size in lanes)
        + tuple(jax.ShapeDtypeStruct(x.shape, x.dtype) for x in (*through, *mixed)),
        in_specs=[vmem] * 2 + [keep] * len(through) + [vmem] * len(mixing),
        out_specs=(vmem,) * parts + (keep,) * len(through) + (pl.BlockSpec(memory_space=pltpu.HBM),) * extra,
        input_output_aliases={2 + i: parts + i for i in range(len(through))},
        scratch_shapes=[pltpu.VMEM(x.shape, BF) for x in mixed] + [pltpu.SemaphoreType.DMA] * extra,
        compiler_params=pltpu.CompilerParams(vmem_limit_bytes=8 * 1024 * 1024),
        cost_estimate=pl.CostEstimate(
            flops=4 * TILE * rows * (high - low), bytes_accessed=8 * TILE * F + 4 * rows * F, transcendentals=0
        ),
        name="weight_blocks",
    )(mine, met, *through, *mixing)


def small_call(kernel, name, outs, operands, after=()):
    n, m = len(operands), len(after)

    def body(*refs):
        kernel(*refs[:n], *refs[n + m :])

    moved = sum(x.size * x.dtype.itemsize for x in (*operands, *outs))
    vmem = pl.BlockSpec(memory_space=pltpu.VMEM)
    return pl.pallas_call(
        body,
        out_shape=tuple(outs),
        in_specs=[vmem] * n + [pl.BlockSpec(memory_space=pl.ANY)] * m,
        out_specs=(vmem,) * len(outs),
        compiler_params=pltpu.CompilerParams(vmem_limit_bytes=2 * moved + 4 * 1024 * 1024),
        cost_estimate=pl.CostEstimate(flops=0, bytes_accessed=0, transcendentals=0),
        name=name,
    )(*operands, *after)


def added(keep, came, halves, after):
    n, lanes = keep.shape
    half = n // 2

    def kernel(keep_ref, came_ref, *outs):
        if halves:
            outs[0][...] = (keep_ref[half:].astype(FP) + came_ref[half:].astype(FP)).astype(BF)
            outs[1][...] = keep_ref[:half].astype(FP) + came_ref[:half].astype(FP)
        else:
            outs[0][...] = (keep_ref[...].astype(FP) + came_ref[...].astype(FP)).astype(BF)

    if halves:
        outs = (jax.ShapeDtypeStruct((half, lanes), BF), jax.ShapeDtypeStruct((half, lanes), FP))
    else:
        outs = (jax.ShapeDtypeStruct((n, lanes), BF),)
    return small_call(kernel, "added", outs, (keep, came), after)


def node_values(keep, came, gains, w_in, w_out, cotangent):
    n = keep.shape[0]

    def kernel(keep_ref, came_ref, gains_ref, w_in_ref, w_out_ref, cot_ref, agg_ref, mine_ref, away_ref, act_ref, gh_ref):
        aggregate = keep_ref[...] + came_ref[...].astype(FP)
        agg_ref[...] = aggregate
        center = jnp.mean(aggregate, axis=-1, keepdims=True)
        spread = jnp.mean(jnp.square(aggregate - center), axis=-1, keepdims=True)
        inverse = lax.rsqrt(spread + 1e-05)
        scaled = ((aggregate - center) * inverse * gains_ref[...]).astype(BF)
        cot = cot_ref[...]
        grad_act = lax.dot_general(cot, w_out_ref[...], (((1,), (1,)), ((), ())), preferred_element_type=FP)
        hidden = jnp.dot(scaled, w_in_ref[...], preferred_element_type=FP)
        sigmoid_h = jax.nn.sigmoid(hidden)
        activated = (hidden * sigmoid_h).astype(BF)
        grad_hidden = (grad_act * sigmoid_h * (1.0 + hidden * (1.0 - sigmoid_h))).astype(BF)
        act_ref[...] = activated
        gh_ref[...] = grad_hidden

        def put(for_in, for_out):
            for_in[:, :F] = scaled
            for_in[:, F:] = grad_hidden
            for_out[:, :F] = cot
            for_out[:, F:] = activated

        first = lax.axis_index("col") & 1 == 0

        @pl.when(first)
        def _():
            put(mine_ref, away_ref)

        @pl.when(jnp.logical_not(first))
        def _():
            put(away_ref, mine_ref)

    outs = (jax.ShapeDtypeStruct((n, F), FP),) + tuple(jax.ShapeDtypeStruct((n, w * F), BF) for w in (3, 3, 2, 2))
    return small_call(kernel, "node_values", outs, (keep, came, gains, w_in, w_out, cotangent))


def joined(held, came, after):
    n, lanes = held.shape

    def kernel(held_ref, came_ref, out_ref):
        out_ref[:n] = held_ref[...]
        out_ref[n:] = came_ref[...]

    outs = (jax.ShapeDtypeStruct((2 * n, lanes), BF),)
    return small_call(kernel, "joined", outs, (held, came), after)[0]


def product(block, rows, first):
    n = block.shape[0] - first

    def kernel(block_ref, rows_ref, out_ref):
        out_ref[...] = jnp.dot(block_ref[first:], rows_ref[...], preferred_element_type=FP)

    return small_call(kernel, "product", (jax.ShapeDtypeStruct((n, F), FP),), (block, rows))[0]


def stacked(pieces, after):
    n = sum(x.shape[0] for x in pieces)

    def kernel(*refs):
        out_ref = refs[-1]
        at = 0
        for x in refs[:-1]:
            out_ref[at : at + x.shape[0]] = x[...]
            out_ref[n + at : n + at + x.shape[0]] = x[...]
            at += x.shape[0]

    return small_call(kernel, "stacked", (jax.ShapeDtypeStruct((2 * n, F), BF),), tuple(pieces), after)[0]


def shards(
    features,
    tile_vals,
    tile_row,
    tile_col,
    tile_count,
    node_type,
    type_gain,
    w_in,
    w_out,
    cotangent,
):
    n_row, n_col = lax.axis_size("row"), lax.axis_size("col")
    n_z = n_col // 2
    row_bits, z_bits = n_row.bit_length() - 1, n_z.bit_length() - 1
    total_nodes = TILE * n_row * n_col
    row, col = lax.axis_index("row"), lax.axis_index("col")
    core, z = col & 1, col >> 1

    def row_step(x, step):
        return exchange(x, n_row, n_col, (1 << step, 1 << (row_bits - 1 - step)), (0, 0))

    def z_step(x, step):
        return exchange(x, n_row, n_col, (0, 0), (1 << step, 1 << (z_bits - 1 - step)))

    def dot(a, b, dims):
        return lax.dot_general(a, b, (dims, ((), ())), preferred_element_type=FP)

    def place(q):
        return row ^ jnp.where(core == 0, q, reversed_bits(q, row_bits))

    here = [features]
    for q in range(1, n_row):
        here.append(exchange(features, n_row, n_col, (q, reversed_bits(q, row_bits)), (0, 0)))
    there = [swap_cores(x, n_row, n_col) for x in here]
    near, far = build(tile_vals, tile_row, tile_col, tile_count, n_row, n_col)
    far = swap_cores(far, n_row, n_col)
    onehot = (node_type[:, None] == jnp.arange(TYPES, dtype=jnp.int32)[None, :]).astype(FP)
    gains = jnp.dot(onehot, type_gain, precision=lax.Precision.HIGHEST)

    mid = near.shape[0] // 2
    here = jnp.concatenate(here + here, axis=0)
    part = product(near, here, mid)
    there = stacked(there, (part,))
    sent = rounded(part + dot(far[mid:], there, ((1,), (0,))))
    total = dot(near[:mid], here, ((1,), (0,))) + dot(far[:mid], there, ((1,), (0,)))
    for step in reversed(range(z_bits)):
        came = z_step(sent, step)
        if step:
            sent, total = added(total, came, True, ())
    aggregate, mine, away, activated, grad_hidden = node_values(total, came, gains, w_in, w_out, cotangent)

    met = swap_cores(away, n_row, n_col)
    node_rows = node_gradients(grad_hidden, w_in, aggregate, gains, cotangent, onehot.T)
    parts = 2
    sizes = (2 * TILE, 2 * TILE)
    lanes = [(sum(sizes[:i]), sizes[i]) for i in range(parts)]
    ahead, behind = range(n_row // 2, n_row), range(n_row // 2)
    first, node_rows = weight_blocks(mine, met, ahead, n_row, lanes[:1], BF, (node_rows,))
    sent = [first] + [weight_blocks(mine, met, ahead, n_row, [x], BF)[0] for x in lanes[1:]]
    *sums, mixed = weight_blocks(mine, met, behind, n_row, lanes, FP, (), (aggregate, activated, w_out))

    grad_rows, gain = node_rows[:TILE], node_rows[TILE:]
    for step in range(z_bits):
        came = z_step(jnp.concatenate([grad_rows, gain], axis=0), step)
        size = grad_rows.shape[0]
        grad_rows = jnp.concatenate([grad_rows, came[:size]], axis=0)
        gain = split(whole(gain) + whole(came[size:]))
    own = n_row * TILE
    came = swap_cores(rounded(dot(far[:, :own], grad_rows, ((0,), (0,)))), n_row, n_col)
    low = dot(near[:, :own], grad_rows, ((0,), (0,))) + came.astype(FP)
    marks = []
    tiles = [low[q * TILE : (q + 1) * TILE] for q in range(n_row)]
    for step in range(row_bits):
        marks.append(jnp.concatenate([rounded(x) for x in tiles[1::2]] + [gain], axis=0))
        came = row_step(marks[-1], step)
        tiles = [x + came[i * TILE : (i + 1) * TILE].astype(FP) for i, x in enumerate(tiles[0::2])]
        gain = split(whole(gain) + whole(came[len(tiles) * TILE :]))
    grad_x = tiles[0]

    for step in reversed(range(row_bits)):
        for i in range(parts):
            mid = sums[i].shape[0] // 2
            came = row_step(sent[i], step)
            sums[i] = sums[i] + came.astype(FP)
            if step:
                sums[i], sent[i] = sums[i][:mid], rounded(sums[i][mid:])
    for step in range(z_bits):
        for i in range(parts):
            if step == 0:
                sent[i] = rounded(sums[i])
            came = z_step(sent[i], z_bits - 1 - step)
            if step == 0 and i == parts - 1:
                sent[i] = added(sent[i], came, False, marks[:1])[0]
            else:
                sent[i] = rounded(sent[i].astype(FP) + came.astype(FP))
    for step in range(row_bits - 1):
        for i in range(parts):
            came = row_step(sent[i], step)
            if step == row_bits - 2:
                sent[i] = joined(sent[i], came, marks[-1:] if i == 0 else sent[:1])
            else:
                sent[i] = jnp.concatenate([sent[i], came], axis=0)
    came = [row_step(x, row_bits - 1) for x in sent]

    factor = float(total_nodes) ** (-0.5)
    others = [swap_cores(x, n_row, n_col) for x in sent]
    gains = [gain, swap_cores(gain, n_row, n_col)]
    half = n_row // 2
    *weights, grad_gain, came[0] = write_weights(sent, others, [], gains, 0, 0, n_row, factor, came[:1], [grad_x])
    others = [swap_cores(x, n_row, n_col) for x in came]
    for i in range(parts - 1):
        weights = write_weights(came[i : i + 1], others[i : i + 1], weights, [], half, lanes[i][0], n_row, factor)
    weights = write_weights(came[-1:], others[-1:], weights, [], half, lanes[-1][0], n_row, factor)
    grad_w_in, grad_w_out = weights
    return mixed, grad_x, grad_w_in, grad_w_out, grad_gain


def solution(mesh):
    return jax.shard_map(
        shards,
        mesh=mesh,
        in_specs=(
            P(("col", "row"), None),
            P("row", "col", None, None),
            P("row", "col"),
            P("row", "col"),
            P("row", "col"),
            P(("row", "col")),
            P(),
            P(),
            P(),
            P(("row", "col"), None),
        ),
        out_specs=(P(("row", "col"), None), P(("col", "row"), None), P(), P(), P()),
        check_vma=False,
    )
```
